128 devices in a mesh: row: 8 (over x, y_hi), col: 16 (over y_lo, z, core).
Axes of the slice: x: 4, y: 4 (y_hi: 2, y_lo: 2; y = y_hi * 2 + y_lo), z: 4, core: 2. Of those that a mesh axis runs over, the one named last changes fastest.
Arguments:
- selected_inverse: bfloat16 [20480, 20480], P('row', 'col'), may hold values from -6 to 6
- pattern: int32 [160, 160], P('row', 'col'), may hold values 0 or 1
- ltil: bfloat16 [20480, 2048], P('row', 'col'), may hold values from -0.0390625 to 0.0390625
- diag_inverse: float32 [2048, 2048], P('row', 'col'), may hold values from -6 to 6
Outputs:
- panel: bfloat16 [20480, 2048], P('row', 'col')
- corner: float32 [2048, 2048], P('row', 'col')
The draws below stay inside these ranges and needn't reach their ends.
All inputs are finite; a program needn't handle non-finite values. No bound on the sum of `pattern` on one device may be relied on, other than what follows from the above.
Results may differ from the reference program's by a relative error of at most 0.0021.
Values may be sent and summed in bfloat16 or wider, within the bound.
A program may use at most 128 MiB of HBM per device.

```python
import jax
import jax.numpy as jnp

W = 2048
BLK = 128
M = 20480
NB = 160


def set_ends(entries, own_key, smallest, largest):
    place = [jax.random.randint(jax.random.fold_in(own_key, axis), (), 0, length) for axis, length in enumerate(entries.shape)]
    widest = entries.shape.index(max(entries.shape))
    beside = place[:widest] + [(place[widest] + 1) % entries.shape[widest]] + place[widest + 1:]
    return entries.at[tuple(place)].set(smallest).at[tuple(beside)].set(largest)


def steps_of(key, shape, cuts, low, top_value):
    def one(dim, parts):
        steps = jax.random.uniform(jax.random.fold_in(jax.random.fold_in(key, 6), dim), (parts,), jnp.float32, low / len(cuts), top_value / len(cuts))
        return jnp.repeat(jnp.exp(steps), shape[dim] // parts).reshape((-1,) + (1,) * (len(shape) - dim - 1))

    loudness = one(*cuts[0])
    for cut in cuts[1:]:
        loudness = loudness * one(*cut)
    return loudness


def gaussian(stream_key, dims, scale, bound, pieces=(), dtype=jnp.bfloat16):
    values = scale * jax.random.normal(stream_key, dims, jnp.float32)
    if pieces:
        values = values * steps_of(stream_key, dims, pieces, -0.22, 0.18)
    return jnp.clip(values, -bound, bound).astype(dtype)


def setup_inputs(seed: int = 0) -> dict:
    seeds = jax.random.split(jax.random.key(seed), 5)
    return {
        "selected_inverse": gaussian(seeds[0], (M, M), 1.0, 6.0, ((0, 8), (1, 16))),
        "pattern": set_ends((jax.random.randint(seeds[1], (NB, NB), 0, 4) < 3).astype(jnp.int32), jax.random.fold_in(seeds[1], 1), 0, 1),
        "ltil": gaussian(seeds[2], (M, W), M ** -0.5, 0.0390625, ((0, 8), (1, 16))),
        "diag_inverse": gaussian(seeds[3], (W, W), 1.0, 6.0, ((0, 8), (1, 16)), jnp.float32),
    }


def reference(selected_inverse, pattern, ltil, diag_inverse):
    rows_all = selected_inverse.shape[0]
    blocks = pattern.shape[0]
    masked = (selected_inverse.reshape(blocks, BLK, blocks, BLK) * pattern[:, None, :, None].astype(jnp.bfloat16)).reshape(rows_all, rows_all)
    total = jnp.dot(masked, ltil, preferred_element_type=jnp.float32)
    panel = (-total).astype(jnp.bfloat16)
    corner = diag_inverse - jnp.dot(ltil.T, panel, preferred_element_type=jnp.float32)
    return panel, corner
```

```python
import functools

import jax
import jax.numpy as jnp
from jax import lax
from jax.experimental import pallas as pl
from jax.experimental.pallas import tpu as pltpu
from jax.sharding import PartitionSpec as P

MESH = pl.DeviceIdType.MESH
BLK = 128
ROWS = 2560
HALF = 1280
TILE = 512
PACKED = 16
F32 = jnp.float32


def device(r, c, k):
    return (r, c * 2 + k)


def kernel(
    a_ref, pat_ref, lt_ref, diag_ref,
    panel_ref, corner_ref,
    a_all, b_all, total, q_out, q_in, mine, slabs, part, parts_in,
    a_sem, core_send, core_recv, first_send, first_recv, pair_send, pair_recv,
    x_send, x_recv, sum_send, sum_recv, slab_send, slab_recv, part_send, part_recv,
):
    r = lax.axis_index("row")
    col = lax.axis_index("col")
    c, k = col // 2, col % 2
    x, yh = r // 2, r % 2
    yl, z = c // 4, c % 4

    def xor(a, b, bits):
        out = 0
        for i in range(bits):
            w = 1 << i
            out = out + w * (((a // w) + (b // w)) % 2)
        return out

    rc = xor(r, c, 3)
    ahead = {1: (x + 1) % 4, 2: (x + 3) % 4, 3: (x + 2) % 4}
    behind = {1: (x + 3) % 4, 2: (x + 1) % 4, 3: (x + 2) % 4}

    barrier = pltpu.get_barrier_semaphore()
    senders = [device(c, rc, k), device(r, c, 1 - k), device(x * 2 + 1 - yh, c, k)]
    senders += [device(behind[d] * 2 + yh, c, k) for d in (1, 2, 3)]
    for i in range(1, 8):
        senders.append(device(r, ((yl + i // 4) % 2) * 4 + (z + 4 - i % 4) % 4, k))
    for b in range(8):
        for kk in range(2):
            senders.append(device(xor(c, b, 3), b, kk))
    for s in senders:
        pl.semaphore_signal(barrier, inc=1, device_id=s, device_id_type=MESH)

    own_a = pltpu.make_async_copy(a_ref, a_all.at[k], a_sem.at[0])
    own_a.start()
    pl.semaphore_wait(barrier, len(senders))

    def remote(src, dst, send, recv, to):
        return pltpu.make_async_remote_copy(
            src_ref=src, dst_ref=dst, send_sem=send, recv_sem=recv, device_id=to, device_id_type=MESH
        )

    stays = jnp.logical_and(r == 0, c == 0)
    first = remote(lt_ref, b_all.at[0], first_send.at[0], first_recv.at[0], device(rc, r, k))

    @pl.when(jnp.logical_not(stays))
    def _():
        first.start()

    @pl.when(stays)
    def _():
        pltpu.make_async_copy(lt_ref, b_all.at[0], first_recv.at[0]).start()

    own_a.wait()

    def mask(i, carry):
        rows = pl.ds(pl.multiple_of(i * BLK, BLK), BLK)
        for j in range(HALF // BLK):
            keep = jnp.full((BLK, BLK), pat_ref[i, j].astype(F32), F32).astype(jnp.bfloat16)
            cols = slice(j * BLK, (j + 1) * BLK)
            a_all[k, rows, cols] = a_all[k, rows, cols] * keep
        return carry

    lax.fori_loop(0, ROWS // BLK, mask, 0)
    swap = remote(a_all.at[k], a_all.at[k], core_send.at[0], core_recv.at[0], device(r, c, 1 - k))
    swap.start()

    first.wait_recv()
    pair = remote(b_all.at[0], b_all.at[1], pair_send.at[0], pair_recv.at[0], device(x * 2 + 1 - yh, c, k))
    pair.start()
    gather = {}
    for d in (1, 2, 3):
        for h in range(2):
            gather[d, h] = remote(
                b_all.at[h], b_all.at[2 * d + h], x_send.at[2 * (d - 1) + h], x_recv.at[2 * (d - 1) + h],
                device(ahead[d] * 2 + yh, c, k),
            )
    gather[1, 0].start()
    gather[2, 0].start()
    pair.wait_recv()
    gather[1, 1].start()
    gather[2, 1].start()
    gather[3, 0].start()
    gather[3, 1].start()

    remote(a_all.at[1 - k], a_all.at[1 - k], core_send.at[0], core_recv.at[0], device(r, c, 1 - k)).wait_recv()

    def slab_of(d, h):
        row = (x if d == 0 else behind[d]) * 2 + (yh if h == 0 else 1 - yh)
        return xor(row, c, 3)

    def send_of(i, dst_col):
        return remote(q_out.at[i], q_in.at[i], sum_send.at[i], sum_recv.at[i], device(r, dst_col, k))

    for d in range(4):
        if d:
            gather[d, 0].wait_recv()
            gather[d, 1].wait_recv()
        right = [
            jnp.concatenate([b_all[2 * d, s, :], b_all[2 * d + 1, s, :]], axis=1)
            for s in (slice(0, HALF), slice(HALF, ROWS))
        ]

        def multiply(t, most, right=right):
            rows = pl.ds(pl.multiple_of(t * TILE, TILE), TILE)
            out = jnp.dot(a_all[0, rows, :], right[0], preferred_element_type=F32)
            out = out + jnp.dot(a_all[1, rows, :], right[1], preferred_element_type=F32)
            total[rows, :] = out
            return jnp.maximum(most, jnp.max(jnp.abs(out), axis=0, keepdims=True))

        most = lax.fori_loop(0, ROWS // TILE, multiply, jnp.zeros((1, 2 * BLK), F32))
        power = jnp.clip(jnp.floor(jnp.log2(32000.0 / most)), -120.0, 120.0)
        scale = jnp.exp2(power)
        slot = []
        for h in range(2):
            s = slab_of(d, h)
            slot.append(((yl + s // 4) % 2) * 4 + (s % 4 + 4 - z) % 4)

        def narrow(t, carry, scale=scale, slot=slot):
            rows = pl.ds(pl.multiple_of(t * TILE, TILE), TILE)
            scaled = (total[rows, :] * scale).astype(jnp.int32).astype(jnp.int16)
            for h in range(2):
                q_out[slot[h], rows, :] = scaled[:, h * BLK:(h + 1) * BLK]
            return carry

        lax.fori_loop(0, ROWS // TILE, narrow, 0)
        code = jnp.broadcast_to(power, (PACKED, 2 * BLK)).astype(jnp.int32).astype(jnp.int16)
        for h in range(2):
            q_out[slot[h], ROWS:, :] = code[:, h * BLK:(h + 1) * BLK]
            @pl.when(slot[h] != 0)
            def _(h=h, d=d):
                send_of(slot[h], slab_of(d, h)).start()

    for i in range(1, 8):
        send_of(i, c).wait_recv()

    def unit(ref, i):
        return jnp.exp2(-ref[i, ROWS:, :].astype(jnp.int32).astype(F32)[0:1, :])

    units = [unit(q_out, 0)] + [unit(q_in, i) for i in range(1, 8)]

    def add(t, carry):
        rows = pl.ds(pl.multiple_of(t * BLK, BLK), BLK)
        out = q_out[0, rows, :].astype(jnp.int32).astype(F32) * units[0]
        for i in range(1, 8):
            out = out + q_in[i, rows, :].astype(jnp.int32).astype(F32) * units[i]
        mine[rows, :] = (-out).astype(jnp.bfloat16)
        panel_ref[rows, :] = (-out).astype(jnp.bfloat16)
        return carry

    lax.fori_loop(0, ROWS // BLK, add, 0)

    third = remote(mine, slabs.at[k], slab_send.at[0], slab_recv.at[0], device(rc, r, k))

    @pl.when(jnp.logical_not(stays))
    def _():
        third.start()

    @pl.when(stays)
    def _():
        pltpu.make_async_copy(mine, slabs.at[k], slab_recv.at[0]).start()

    third.wait_recv()
    share = remote(slabs.at[k], slabs.at[k], slab_send.at[1], slab_recv.at[1], device(r, c, 1 - k))
    share.start()
    remote(slabs.at[1 - k], slabs.at[1 - k], slab_send.at[1], slab_recv.at[1], device(r, c, 1 - k)).wait_recv()

    def corner_of(j, kk):
        to = slab_of(j // 2, j % 2)
        own = jnp.logical_and(jnp.logical_and(to == r, rc == c), k == kk)
        copy = remote(
            part.at[j, kk], parts_in.at[c, k], part_send.at[j, kk], part_recv.at[c, k], device(to, rc, kk)
        )
        return own, copy

    for j in range(8):
        for kk in range(2):
            part[j, kk] = lax.dot_general(
                b_all[j], slabs[kk], (((0,), (0,)), ((), ())), preferred_element_type=F32
            )
            own, copy = corner_of(j, kk)

            @pl.when(own)
            def _(j=j, kk=kk):
                parts_in[c, k] = part[j, kk]

            @pl.when(jnp.logical_not(own))
            def _(copy=copy):
                copy.start()

    for kk in range(2):
        rows = slice(kk * BLK, (kk + 1) * BLK)
        out = diag_ref[rows, :]
        for b in range(8):
            own = jnp.logical_and(jnp.logical_and(xor(c, b, 3) == r, c == b), k == kk)

            @pl.when(jnp.logical_not(own))
            def _(b=b, kk=kk):
                remote(
                    part.at[0, 0], parts_in.at[b, kk], part_send.at[0, 0], part_recv.at[b, kk], device(r, c, 1 - k)
                ).wait_recv()

            out = out - parts_in[b, kk]
        corner_ref[rows, :] = out

    @pl.when(jnp.logical_not(stays))
    def _():
        first.wait_send()
        third.wait_send()

    swap.wait_send()
    pair.wait_send()
    share.wait_send()
    for d in (1, 2, 3):
        for h in range(2):
            gather[d, h].wait_send()
    for i in range(1, 8):
        send_of(i, c).wait_send()
    for j in range(8):
        for kk in range(2):
            own, copy = corner_of(j, kk)

            @pl.when(jnp.logical_not(own))
            def _(copy=copy):
                copy.wait_send()


def local(selected_inverse, pattern, ltil, diag_inverse):
    dma = pltpu.SemaphoreType.DMA
    vmem, anywhere = pl.BlockSpec(memory_space=pltpu.VMEM), pl.BlockSpec(memory_space=pl.ANY)
    return pl.pallas_call(
        kernel,
        out_shape=(
            jax.ShapeDtypeStruct((ROWS, BLK), jnp.bfloat16),
            jax.ShapeDtypeStruct((2 * BLK, BLK), F32),
        ),
        in_specs=[anywhere, pl.BlockSpec(memory_space=pltpu.SMEM), anywhere, vmem],
        out_specs=(vmem, vmem),
        scratch_shapes=[
            pltpu.VMEM((2, ROWS, HALF), jnp.bfloat16),
            pltpu.VMEM((8, ROWS, BLK), jnp.bfloat16),
            pltpu.VMEM((ROWS, 2 * BLK), F32),
            pltpu.VMEM((8, ROWS + PACKED, BLK), jnp.int16),
            pltpu.VMEM((8, ROWS + PACKED, BLK), jnp.int16),
            pltpu.VMEM((ROWS, BLK), jnp.bfloat16),
            pltpu.VMEM((2, ROWS, BLK), jnp.bfloat16),
            pltpu.VMEM((8, 2, BLK, BLK), F32),
            pltpu.VMEM((8, 2, BLK, BLK), F32),
            dma((1,)), dma((1,)), dma((1,)), dma((1,)), dma((1,)), dma((1,)), dma((1,)),
            dma((6,)), dma((6,)), dma((8,)), dma((8,)), dma((2,)), dma((2,)), dma((8, 2)), dma((8, 2)),
        ],
        compiler_params=pltpu.CompilerParams(
            collective_id=0, has_side_effects=True, vmem_limit_bytes=56 * 1024 * 1024
        ),
        cost_estimate=pl.CostEstimate(flops=15_000_000_000, bytes_accessed=20_000_000, transcendentals=0),
    )(selected_inverse, pattern, ltil, diag_inverse)


def solution(mesh):
    placed = (P("row", "col"), P("row", "col"), P("row", "col"), P("row", "col"))
    return jax.shard_map(
        local,
        mesh=mesh,
        in_specs=placed,
        out_specs=(P("row", "col"), P("row", "col")),
        check_vma=False,
    )
```

```python
import jax
import jax.numpy as jnp
from jax import lax
from jax.experimental import pallas as pl
from jax.experimental.pallas import tpu as pltpu
from jax.sharding import PartitionSpec as P

MESH = pl.DeviceIdType.MESH
BLK = 128
ROWS = 2560
HALF = 1280
TILE = 640
TILES = 4
CODE = 16
F32 = jnp.float32
BF16 = jnp.bfloat16


def device(r, c, k):
    return (r, c * 2 + k)


def xor(a, b, bits):
    out = 0
    for i in range(bits):
        w = 1 << i
        out = out + w * (((a // w) + (b // w)) % 2)
    return out


def swizzle(c):
    return (c // 4) * 4 + ((c // 2 + c // 4) % 2) * 2 + c % 2


def code_of(most):
    return jnp.clip(jnp.floor(jnp.log2(32000.0 / most)), -120.0, 120.0)


def as_int16(values):
    return values.astype(jnp.int32).astype(jnp.int16)


def as_float(values):
    return values.astype(jnp.int32).astype(F32)


def unit_of(code):
    return jnp.exp2(-as_float(code)[0:1, :])


def kernel(
    a_ref, pat_ref, lt_ref, diag_ref,
    panel_ref, corner_ref,
    pat, a_all, b_all, b_turned, z_out, z_in, y_out, y_in, late_in, slabs, part, parts_in,
    a_sem, core_send, core_recv, first_send, first_recv, pair_send, pair_recv,
    x_send, x_recv, z_send, z_recv, y_send, y_recv, late_send, late_recv,
    slab_send, slab_recv, share_send, share_recv, part_send, part_recv,
):
    r = lax.axis_index("row")
    col = lax.axis_index("col")
    c, k = col // 2, col % 2
    x, yh = r // 2, r % 2
    yl, z = c // 4, c % 4
    home = xor(r, swizzle(c), 3)
    slab = swizzle(xor(r, c, 3))
    x_of = {0: x, 1: (x + 3) % 4, 2: (x + 1) % 4, 3: (x + 2) % 4}
    x_ahead = device(x_of[2] * 2 + yh, c, k)
    x_back = device(x_of[1] * 2 + yh, c, k)
    partner = device(x * 2 + 1 - yh, c, k)
    other = device(r, c, 1 - k)

    barrier = pltpu.get_barrier_semaphore()
    senders = [device(c, swizzle(xor(r, c, 3)), k), other, partner, x_ahead, x_back]
    for i in range(1, 8):
        senders.append(device(r, ((yl + i // 4) % 2) * 4 + xor(z, i % 4, 2), k))
    for b in range(8):
        for kk in range(2):
            senders.append(device(xor(swizzle(c), b, 3), b, kk))
    for s in senders:
        pl.semaphore_signal(barrier, inc=1, device_id=s, device_id_type=MESH)

    own_a = pltpu.make_async_copy(a_ref, a_all.at[k], a_sem.at[0])
    own_a.start()
    own_pat = pltpu.make_async_copy(pat_ref, pat, a_sem.at[1])
    own_pat.start()
    pl.semaphore_wait(barrier, len(senders))

    def remote(src, dst, send, recv, to):
        return pltpu.make_async_remote_copy(
            src_ref=src, dst_ref=dst, send_sem=send, recv_sem=recv, device_id=to, device_id_type=MESH
        )

    stays = jnp.logical_and(r == 0, c == 0)
    halves = [pl.ds(q * HALF, HALF) for q in range(2)]
    first = [
        remote(lt_ref.at[rows], b_all.at[0, rows], first_send.at[q], first_recv.at[q], device(home, r, k))
        for q, rows in enumerate(halves)
    ]

    @pl.when(jnp.logical_not(stays))
    def _():
        for copy in first:
            copy.start()

    @pl.when(stays)
    def _():
        for q, rows in enumerate(halves):
            pltpu.make_async_copy(lt_ref.at[rows], b_all.at[0, rows], first_recv.at[q]).start()

    own_a.wait()
    own_pat.wait()

    def mask(i, carry):
        rows = pl.ds(pl.multiple_of(i * BLK, BLK), BLK)
        for j in range(HALF // BLK):
            keep = jnp.full((BLK, BLK), pat[i, j].astype(F32), F32).astype(BF16)
            cols = slice(j * BLK, (j + 1) * BLK)
            a_all[k, rows, cols] = a_all[k, rows, cols] * keep
        return carry

    lax.fori_loop(0, ROWS // BLK, mask, 0)
    swap = remote(a_all.at[k], a_all.at[k], core_send.at[0], core_recv.at[0], other)
    swap.start()

    def piece(s, q):
        return b_all.at[s, pl.ds(q * HALF, HALF)]

    def along(d, h, q):
        if (d, h) == (3, 1):
            source, to = 6, partner
        else:
            source = {1: h, 2: h, 3: 2 if q == 0 else 4}[d]
            to = x_ahead if d == 1 or (d == 3 and q == 0) else x_back
        i = (d - 1) * 4 + h * 2 + q
        return remote(piece(source, q), piece(2 * d + h, q), x_send.at[i], x_recv.at[i], to)

    def spread(h, q):
        along(1, h, q).start()
        along(2, h, q).start()

    pair = [remote(piece(0, q), piece(1, q), pair_send.at[q], pair_recv.at[q], partner) for q in range(2)]
    for q in range(2):
        first[q].wait_recv()
        spread(0, q)
        pair[q].start()

    remote(a_all.at[1 - k], a_all.at[1 - k], core_send.at[0], core_recv.at[0], other).wait_recv()

    def relation(d, h):
        hi, lo = x_of[d] // 2, x_of[d] % 2
        return hi, ((hi + lo + yl) % 2) * 2 + (yh + h) % 2

    def z_copy(i, t):
        return remote(
            z_out.at[i, t], z_in.at[i, t], z_send.at[i, t], z_recv.at[i, t],
            device(r, yl * 4 + xor(z, i % 4, 2), k),
        )

    direct = x < 2
    late_z = [jnp.where(x_of[1] >= 2, relation(1, 1)[1], relation(2, 1)[1]), relation(3, 1)[1]]

    def late(i, t):
        return remote(
            z_out.at[4 + late_z[i], t], late_in.at[i, t], late_send.at[i, t], late_recv.at[i, t],
            device(r, (1 - yl) * 4 + xor(z, late_z[i], 2), k),
        )

    def y_copy(t):
        return remote(y_out.at[t], y_in.at[t], y_send.at[t], y_recv.at[t], device(r, (1 - yl) * 4 + z, k))

    def each_tile(body):
        def run(t, carry):
            body(t)
            return carry

        lax.fori_loop(0, TILES, run, 0)

    def rows_of(t):
        return pl.ds(pl.multiple_of(t * TILE, TILE), TILE)

    def packed(values):
        power = code_of(jnp.max(jnp.abs(values), axis=0, keepdims=True))
        code = as_int16(jnp.broadcast_to(power, (CODE, values.shape[1])))
        return as_int16(values * jnp.exp2(power)), code

    def step(slots):
        right = [
            jnp.concatenate([b_all[2 * d + h, s, :] for d, h in slots], axis=1)
            for s in (slice(0, HALF), slice(HALF, ROWS))
        ]

        to = [relation(d, h) for d, h in slots]
        at = [across * 4 + by for across, by in to]

        def multiply(t):
            rows = rows_of(t)
            out = jnp.dot(a_all[0, rows, :], right[0], preferred_element_type=F32)
            out = out + jnp.dot(a_all[1, rows, :], right[1], preferred_element_type=F32)
            scaled, code = packed(out)
            for i, slot in enumerate(slots):
                cols = slice(i * BLK, (i + 1) * BLK)
                z_out[at[i], t, 0:TILE, :] = scaled[:, cols]
                z_out[at[i], t, TILE:, :] = code[:, cols]
                moves = to[i][1] != 0
                if slot in ((1, 1), (2, 1), (3, 1)):
                    straight = to[i][0] == 1
                    moves = jnp.logical_and(moves, jnp.logical_not(straight))

                    @pl.when(straight)
                    def _(slot=slot):
                        late(0 if slot != (3, 1) else 1, t).start()

                @pl.when(moves)
                def _(i=i):
                    z_copy(at[i], t).start()

        each_tile(multiply)

    def turn(slots):
        for d, h in slots:
            s = 2 * d + h
            b_turned[s * BLK:(s + 1) * BLK, :] = b_all[s].T

    step([(0, 0)])
    along(1, 0, 0).wait_recv()
    along(3, 0, 0).start()
    pair[0].wait_recv()
    spread(1, 0)
    along(2, 0, 1).wait_recv()
    along(3, 0, 1).start()
    pair[1].wait_recv()
    spread(1, 1)
    step([(0, 1)])
    along(1, 0, 1).wait_recv()
    along(2, 0, 0).wait_recv()
    step([(1, 0), (2, 0)])
    for q in range(2):
        along(3, 0, q).wait_recv()
        along(3, 1, q).start()
    step([(3, 0)])
    turn([(0, 0), (0, 1), (1, 0), (2, 0), (3, 0)])
    for d in (1, 2):
        for q in range(2):
            along(d, 1, q).wait_recv()
    step([(1, 1), (2, 1)])
    for q in range(2):
        along(3, 1, q).wait_recv()
    step([(3, 1)])
    turn([(1, 1), (2, 1), (3, 1)])

    def parts_of(across, t):
        return [z_out.at[across * 4, t]] + [z_in.at[across * 4 + i, t] for i in range(1, 4)]

    def sum_of(refs, used=None):
        out = 0.0
        for i, ref in enumerate(refs):
            unit = unit_of(ref[TILE:, :])
            if used is not None:
                unit = jnp.where(used[i], unit, 0.0)
            out = out + as_float(ref[0:TILE, :]) * unit
        return out

    used_across = [
        jnp.logical_and(late_z[0] != i, jnp.logical_not(jnp.logical_and(direct, late_z[1] == i))) for i in range(4)
    ]

    def pass_on(t):
        for i in range(1, 4):
            @pl.when(used_across[i])
            def _(i=i):
                z_copy(4 + i, t).wait_recv()

        y_out[t, 0:TILE, :], y_out[t, TILE:, :] = packed(sum_of(parts_of(1, t), used_across))
        y_copy(t).start()

    each_tile(pass_on)

    def third(t):
        rows = rows_of(t)
        return remote(panel_ref.at[rows], slabs.at[k, rows], slab_send.at[t], slab_recv.at[t], device(home, r, k))

    def finish(t):
        for i in range(1, 4):
            z_copy(i, t).wait_recv()

        late(0, t).wait_recv()

        @pl.when(direct)
        def _():
            late(1, t).wait_recv()

        y_copy(t).wait_recv()
        rows = rows_of(t)
        out = sum_of(parts_of(0, t) + [y_in.at[t], late_in.at[0, t], late_in.at[1, t]], [True] * 6 + [direct])
        panel_ref[rows, :] = (-out).astype(BF16)

        @pl.when(jnp.logical_not(stays))
        def _():
            third(t).start()

        @pl.when(stays)
        def _():
            pltpu.make_async_copy(panel_ref.at[rows], slabs.at[k, rows], slab_recv.at[t]).start()

    each_tile(finish)

    def share(t, owner):
        rows = rows_of(t)
        return remote(slabs.at[owner, rows], slabs.at[owner, rows], share_send.at[t], share_recv.at[t], other)

    def hand_over(t):
        third(t).wait_recv()
        share(t, k).start()

    each_tile(hand_over)

    def corner_of(j, kk):
        d, h = j // 2, j % 2
        to = swizzle(xor(x_of[d] * 2 + (yh + h) % 2, c, 3))
        own = jnp.logical_and(jnp.logical_and(to == r, slab == c), k == kk)
        i = j * 2 + kk
        copy = remote(
            part.at[i], parts_in.at[c * 2 + k], part_send.at[i], part_recv.at[c * 2 + k], device(to, slab, kk)
        )
        return i, own, copy

    for t in range(TILES):
        share(t, 1 - k).wait_recv()
    right = jnp.concatenate([slabs[0], slabs[1]], axis=1)
    for j in range(8):
        out = jnp.dot(b_turned[j * BLK:(j + 1) * BLK, :], right, preferred_element_type=F32)
        scaled, code = packed(out)
        for kk in range(2):
            i, own, copy = corner_of(j, kk)
            part[i, 0:BLK, :] = scaled[:, kk * BLK:(kk + 1) * BLK]
            part[i, BLK:, :] = code[:, kk * BLK:(kk + 1) * BLK]

            @pl.when(own)
            def _(i=i):
                parts_in[c * 2 + k] = part[i]

            @pl.when(jnp.logical_not(own))
            def _(copy=copy):
                copy.start()

    for kk in range(2):
        rows = slice(kk * BLK, (kk + 1) * BLK)
        out = diag_ref[rows, :]
        for b in range(8):
            i = b * 2 + kk
            own = jnp.logical_and(jnp.logical_and(xor(swizzle(c), b, 3) == r, c == b), k == kk)

            @pl.when(jnp.logical_not(own))
            def _(i=i):
                remote(part.at[0], parts_in.at[i], part_send.at[0], part_recv.at[i], other).wait_recv()

            out = out - as_float(parts_in[i, 0:BLK, :]) * unit_of(parts_in[i, BLK:, :])
        corner_ref[rows, :] = out

    @pl.when(jnp.logical_not(stays))
    def _():
        for copy in first:
            copy.wait_send()

    swap.wait_send()
    for q in range(2):
        pair[q].wait_send()
        for d in (1, 2, 3):
            for h in range(2):
                along(d, h, q).wait_send()

    def drain(t):
        for i in (1, 2, 3, 5, 6, 7):
            @pl.when(True if i < 4 else used_across[i - 4])
            def _(i=i):
                z_copy(i, t).wait_send()

        late(0, t).wait_send()

        @pl.when(direct)
        def _():
            late(1, t).wait_send()

        @pl.when(jnp.logical_not(stays))
        def _():
            third(t).wait_send()

        y_copy(t).wait_send()
        share(t, k).wait_send()

    each_tile(drain)
    for j in range(8):
        for kk in range(2):
            _, own, copy = corner_of(j, kk)

            @pl.when(jnp.logical_not(own))
            def _(copy=copy):
                copy.wait_send()


def local(selected_inverse, pattern, ltil, diag_inverse):
    dma = pltpu.SemaphoreType.DMA
    vmem, anywhere = pl.BlockSpec(memory_space=pltpu.VMEM), pl.BlockSpec(memory_space=pl.ANY)
    return pl.pallas_call(
        kernel,
        out_shape=(
            jax.ShapeDtypeStruct((ROWS, BLK), BF16),
            jax.ShapeDtypeStruct((2 * BLK, BLK), F32),
        ),
        in_specs=[anywhere, anywhere, anywhere, vmem],
        out_specs=(vmem, vmem),
        scratch_shapes=[
            pltpu.SMEM((ROWS // BLK, HALF // BLK), jnp.int32),
            pltpu.VMEM((2, ROWS, HALF), BF16),
            pltpu.VMEM((8, ROWS, BLK), BF16),
            pltpu.VMEM((8 * BLK, ROWS), BF16),
            pltpu.VMEM((8, TILES, TILE + CODE, BLK), jnp.int16),
            pltpu.VMEM((8, TILES, TILE + CODE, BLK), jnp.int16),
            pltpu.VMEM((TILES, TILE + CODE, BLK), jnp.int16),
            pltpu.VMEM((TILES, TILE + CODE, BLK), jnp.int16),
            pltpu.VMEM((2, TILES, TILE + CODE, BLK), jnp.int16),
            pltpu.VMEM((2, ROWS, BLK), BF16),
            pltpu.VMEM((16, BLK + CODE, BLK), jnp.int16),
            pltpu.VMEM((16, BLK + CODE, BLK), jnp.int16),
            dma((2,)), dma((1,)), dma((1,)), dma((2,)), dma((2,)), dma((2,)), dma((2,)),
            dma((12,)), dma((12,)), dma((8, TILES)), dma((8, TILES)), dma((TILES,)), dma((TILES,)),
            dma((2, TILES)), dma((2, TILES)), dma((TILES,)), dma((TILES,)), dma((TILES,)), dma((TILES,)),
            dma((16,)), dma((16,)),
        ],
        compiler_params=pltpu.CompilerParams(
            collective_id=0, has_side_effects=True, vmem_limit_bytes=56 * 1024 * 1024
        ),
        cost_estimate=pl.CostEstimate(flops=15_000_000_000, bytes_accessed=20_000_000, transcendentals=0),
    )(selected_inverse, pattern, ltil, diag_inverse)


def solution(mesh):
    placed = (P("row", "col"), P("row", "col"), P("row", "col"), P("row", "col"))
    return jax.shard_map(
        local,
        mesh=mesh,
        in_specs=placed,
        out_specs=(P("row", "col"), P("row", "col")),
        check_vma=False,
    )
```

```python
import jax
import jax.numpy as jnp
from jax import lax
from jax.experimental import pallas as pl
from jax.experimental.pallas import tpu as pltpu
from jax.sharding import PartitionSpec as P

MESH = pl.DeviceIdType.MESH
BLK = 128
ROWS = 2560
HALF = 1280
TILE = 640
TILES = 4
CODE = 16
F32 = jnp.float32
BF16 = jnp.bfloat16


def device(r, c, k):
    return (r, c * 2 + k)


def xor(a, b, bits):
    out = 0
    for i in range(bits):
        w = 1 << i
        out = out + w * (((a // w) + (b // w)) % 2)
    return out


def swizzle(c):
    return (c // 4) * 4 + ((c // 2 + c // 4) % 2) * 2 + c % 2


def code_of(most):
    return jnp.clip(jnp.floor(jnp.log2(32000.0 / most)), -120.0, 120.0)


def as_int16(values):
    return values.astype(jnp.int32).astype(jnp.int16)


def as_float(values):
    return values.astype(jnp.int32).astype(F32)


def unit_of(code):
    return jnp.exp2(-as_float(code)[0:1, :])


def kernel(
    a_ref, pat_ref, lt_ref, diag_ref,
    panel_ref, corner_ref,
    pat, a_all, b_all, b_turned, z_out, z_in, y_out, y_in, slabs, corner, part, parts_in,
    a_sem, core_send, core_recv, first_send, first_recv, pair_send, pair_recv,
    x_send, x_recv, z_send, z_recv, y_send, y_recv,
    slab_send, slab_recv, share_send, share_recv, part_send, part_recv,
):
    r = lax.axis_index("row")
    col = lax.axis_index("col")
    c, k = col // 2, col % 2
    x, yh = r // 2, r % 2
    yl, z = c // 4, c % 4
    home = xor(r, swizzle(c), 3)
    slab = swizzle(xor(r, c, 3))
    x_of = {0: x, 1: (x + 3) % 4, 2: (x + 1) % 4, 3: (x + 2) % 4}
    x_ahead = device(x_of[2] * 2 + yh, c, k)
    x_back = device(x_of[1] * 2 + yh, c, k)
    partner = device(x * 2 + 1 - yh, c, k)
    other = device(r, c, 1 - k)

    barrier = pltpu.get_barrier_semaphore()
    senders = [device(c, swizzle(xor(r, c, 3)), k), other, partner, x_ahead, x_back]
    for i in range(1, 8):
        senders.append(device(r, ((yl + i // 4) % 2) * 4 + xor(z, i % 4, 2), k))
    for b in range(8):
        for kk in range(2):
            senders.append(device(xor(swizzle(c), b, 3), b, kk))
    for s in senders:
        pl.semaphore_signal(barrier, inc=1, device_id=s, device_id_type=MESH)

    own_a = pltpu.make_async_copy(a_ref, a_all.at[k], a_sem.at[0])
    own_a.start()
    own_pat = pltpu.make_async_copy(pat_ref, pat, a_sem.at[1])
    own_pat.start()
    pl.semaphore_wait(barrier, len(senders))

    def remote(src, dst, send, recv, to):
        return pltpu.make_async_remote_copy(
            src_ref=src, dst_ref=dst, send_sem=send, recv_sem=recv, device_id=to, device_id_type=MESH
        )

    stays = jnp.logical_and(r == 0, c == 0)
    halves = [pl.ds(q * HALF, HALF) for q in range(2)]
    first = [
        remote(lt_ref.at[rows], b_all.at[0, rows], first_send.at[q], first_recv.at[q], device(home, r, k))
        for q, rows in enumerate(halves)
    ]

    @pl.when(jnp.logical_not(stays))
    def _():
        for copy in first:
            copy.start()

    @pl.when(stays)
    def _():
        for q, rows in enumerate(halves):
            pltpu.make_async_copy(lt_ref.at[rows], b_all.at[0, rows], first_recv.at[q]).start()

    own_a.wait()
    own_pat.wait()

    def mask(i, carry):
        rows = pl.ds(pl.multiple_of(i * BLK, BLK), BLK)
        for j in range(HALF // BLK):
            keep = jnp.full((BLK, BLK), pat[i, j].astype(F32), F32).astype(BF16)
            cols = slice(j * BLK, (j + 1) * BLK)
            a_all[k, rows, cols] = a_all[k, rows, cols] * keep
        return carry

    lax.fori_loop(0, ROWS // BLK, mask, 0)
    swap = remote(a_all.at[k], a_all.at[k], core_send.at[0], core_recv.at[0], other)
    swap.start()

    def piece(s, q):
        return b_all.at[s, pl.ds(q * HALF, HALF)]

    def along(d, h, q):
        if (d, h) == (3, 1):
            source, to = 6, partner
        else:
            source = {1: h, 2: h, 3: 2 if q == 0 else 4}[d]
            to = x_ahead if d == 1 or (d == 3 and q == 0) else x_back
        i = (d - 1) * 4 + h * 2 + q
        return remote(piece(source, q), piece(2 * d + h, q), x_send.at[i], x_recv.at[i], to)

    def spread(h, q):
        along(1, h, q).start()
        along(2, h, q).start()

    pair = [remote(piece(0, q), piece(1, q), pair_send.at[q], pair_recv.at[q], partner) for q in range(2)]
    for q in range(2):
        first[q].wait_recv()
        spread(0, q)
        pair[q].start()

    remote(a_all.at[1 - k], a_all.at[1 - k], core_send.at[0], core_recv.at[0], other).wait_recv()

    def relation(d, h):
        hi, lo = x_of[d] // 2, x_of[d] % 2
        return hi, ((hi + lo + yl) % 2) * 2 + (yh + h) % 2

    def z_copy(i, t):
        return remote(
            z_out.at[i, t], z_in.at[i, t], z_send.at[i, t], z_recv.at[i, t],
            device(r, yl * 4 + xor(z, i % 4, 2), k),
        )

    def y_copy(t):
        return remote(y_out.at[t], y_in.at[t], y_send.at[t], y_recv.at[t], device(r, (1 - yl) * 4 + z, k))

    def each_tile(body):
        def run(t, carry):
            body(t)
            return carry

        lax.fori_loop(0, TILES, run, 0)

    def rows_of(t):
        return pl.ds(t * TILE if isinstance(t, int) else pl.multiple_of(t * TILE, TILE), TILE)

    def packed(values):
        power = code_of(jnp.max(jnp.abs(values), axis=0, keepdims=True))
        code = as_int16(jnp.broadcast_to(power, (CODE, values.shape[1])))
        return as_int16(values * jnp.exp2(power)), code

    def step(*groups):
        def multiply(t):
            for slots in groups:
                multiply_group(t, slots)

        def multiply_group(t, slots):
            rows = rows_of(t)
            right = [
                jnp.concatenate([b_all[2 * d + h, s, :] for d, h in slots], axis=1)
                for s in (slice(0, HALF), slice(HALF, ROWS))
            ]
            out = jnp.dot(a_all[0, rows, :], right[0], preferred_element_type=F32)
            out = out + jnp.dot(a_all[1, rows, :], right[1], preferred_element_type=F32)
            scaled, code = packed(out)
            for i, slot in enumerate(slots):
                across, by = relation(*slot)
                at = across * 4 + by
                cols = slice(i * BLK, (i + 1) * BLK)
                z_out[at, t, 0:TILE, :] = scaled[:, cols]
                z_out[at, t, TILE:, :] = code[:, cols]
                @pl.when(by != 0)
                def _(at=at):
                    z_copy(at, t).start()

        each_tile(multiply)

    def turn(slots):
        for d, h in slots:
            s = 2 * d + h
            for t in range(TILES):
                b_turned[t, s * BLK:(s + 1) * BLK, :] = b_all[s, t * TILE:(t + 1) * TILE, :].T

    step([(0, 0)])
    along(1, 0, 0).wait_recv()
    along(3, 0, 0).start()
    pair[0].wait_recv()
    spread(1, 0)
    along(2, 0, 1).wait_recv()
    along(3, 0, 1).start()
    pair[1].wait_recv()
    spread(1, 1)
    step([(0, 1)])
    along(1, 0, 1).wait_recv()
    along(2, 0, 0).wait_recv()
    step([(1, 0), (2, 0)])
    for q in range(2):
        along(3, 0, q).wait_recv()
        along(3, 1, q).start()
    step([(3, 0)])
    turn([(0, 0), (0, 1), (1, 0), (2, 0), (3, 0)])
    for d in (1, 2):
        for q in range(2):
            along(d, 1, q).wait_recv()
    for q in range(2):
        along(3, 1, q).wait_recv()
    step([(1, 1), (2, 1)], [(3, 1)])

    def parts_of(across, t):
        return [z_out.at[across * 4, t]] + [z_in.at[across * 4 + i, t] for i in range(1, 4)]

    def sum_of(refs):
        out = 0.0
        for ref in refs:
            out = out + as_float(ref[0:TILE, :]) * unit_of(ref[TILE:, :])
        return out

    def pass_on(t):
        for i in range(5, 8):
            z_copy(i, t).wait_recv()

        y_out[t, 0:TILE, :], y_out[t, TILE:, :] = packed(sum_of(parts_of(1, t)))
        y_copy(t).start()

    def third(t):
        rows = rows_of(t)
        return remote(panel_ref.at[rows], slabs.at[k, rows], slab_send.at[t], slab_recv.at[t], device(home, r, k))

    def finish(t):
        for i in range(1, 4):
            z_copy(i, t).wait_recv()

        y_copy(t).wait_recv()
        rows = rows_of(t)
        out = sum_of(parts_of(0, t) + [y_in.at[t]])
        panel_ref[rows, :] = (-out).astype(BF16)

        @pl.when(jnp.logical_not(stays))
        def _():
            third(t).start()

        @pl.when(stays)
        def _():
            pltpu.make_async_copy(panel_ref.at[rows], slabs.at[k, rows], slab_recv.at[t]).start()

    for t in range(TILES + 1):
        if t < TILES:
            pass_on(t)
        if t > 0:
            finish(t - 1)
    turn([(1, 1), (2, 1), (3, 1)])

    def share(t, owner):
        rows = rows_of(t)
        return remote(slabs.at[owner, rows], slabs.at[owner, rows], share_send.at[t], share_recv.at[t], other)

    for t in range(TILES + 1):
        if t < TILES:
            third(t).wait_recv()
            share(t, k).start()
        if t > 0:
            share(t - 1, 1 - k).wait_recv()
            rows = slice((t - 1) * TILE, t * TILE)
            right = jnp.concatenate([slabs[0, rows, :], slabs[1, rows, :]], axis=1)
            for j in range(4):
                span = slice(j * 2 * BLK, (j + 1) * 2 * BLK)
                out = jnp.dot(b_turned[t - 1, span, :], right, preferred_element_type=F32)
                corner[span, :] = out if t == 1 else corner[span, :] + out

    def corner_of(j, kk):
        d, h = j // 2, j % 2
        to = swizzle(xor(x_of[d] * 2 + (yh + h) % 2, c, 3))
        own = jnp.logical_and(jnp.logical_and(to == r, slab == c), k == kk)
        i = j * 2 + kk
        copy = remote(
            part.at[i], parts_in.at[c * 2 + k], part_send.at[i], part_recv.at[c * 2 + k], device(to, slab, kk)
        )
        return i, own, copy

    for j in range(8):
        scaled, code = packed(corner[j * BLK:(j + 1) * BLK, :])
        for kk in range(2):
            i, own, copy = corner_of(j, kk)
            part[i, 0:BLK, :] = scaled[:, kk * BLK:(kk + 1) * BLK]
            part[i, BLK:, :] = code[:, kk * BLK:(kk + 1) * BLK]

            @pl.when(own)
            def _(i=i):
                parts_in[c * 2 + k] = part[i]

            @pl.when(jnp.logical_not(own))
            def _(copy=copy):
                copy.start()

    for kk in range(2):
        rows = slice(kk * BLK, (kk + 1) * BLK)
        out = diag_ref[rows, :]
        for b in range(8):
            i = b * 2 + kk
            own = jnp.logical_and(jnp.logical_and(xor(swizzle(c), b, 3) == r, c == b), k == kk)

            @pl.when(jnp.logical_not(own))
            def _(i=i):
                remote(part.at[0], parts_in.at[i], part_send.at[0], part_recv.at[i], other).wait_recv()

            out = out - as_float(parts_in[i, 0:BLK, :]) * unit_of(parts_in[i, BLK:, :])
        corner_ref[rows, :] = out

    @pl.when(jnp.logical_not(stays))
    def _():
        for copy in first:
            copy.wait_send()

    swap.wait_send()
    for q in range(2):
        pair[q].wait_send()
        for d in (1, 2, 3):
            for h in range(2):
                along(d, h, q).wait_send()

    def drain(t):
        for i in (1, 2, 3, 5, 6, 7):
            z_copy(i, t).wait_send()


        @pl.when(jnp.logical_not(stays))
        def _():
            third(t).wait_send()

        y_copy(t).wait_send()
        share(t, k).wait_send()

    each_tile(drain)
    for j in range(8):
        for kk in range(2):
            _, own, copy = corner_of(j, kk)

            @pl.when(jnp.logical_not(own))
            def _(copy=copy):
                copy.wait_send()


def local(selected_inverse, pattern, ltil, diag_inverse):
    dma = pltpu.SemaphoreType.DMA
    vmem, anywhere = pl.BlockSpec(memory_space=pltpu.VMEM), pl.BlockSpec(memory_space=pl.ANY)
    return pl.pallas_call(
        kernel,
        out_shape=(
            jax.ShapeDtypeStruct((ROWS, BLK), BF16),
            jax.ShapeDtypeStruct((2 * BLK, BLK), F32),
        ),
        in_specs=[anywhere, anywhere, anywhere, vmem],
        out_specs=(vmem, vmem),
        scratch_shapes=[
            pltpu.SMEM((ROWS // BLK, HALF // BLK), jnp.int32),
            pltpu.VMEM((2, ROWS, HALF), BF16),
            pltpu.VMEM((8, ROWS, BLK), BF16),
            pltpu.VMEM((TILES, 8 * BLK, TILE), BF16),
            pltpu.VMEM((8, TILES, TILE + CODE, BLK), jnp.int16),
            pltpu.VMEM((8, TILES, TILE + CODE, BLK), jnp.int16),
            pltpu.VMEM((TILES, TILE + CODE, BLK), jnp.int16),
            pltpu.VMEM((TILES, TILE + CODE, BLK), jnp.int16),
            pltpu.VMEM((2, ROWS, BLK), BF16),
            pltpu.VMEM((8 * BLK, 2 * BLK), F32),
            pltpu.VMEM((16, BLK + CODE, BLK), jnp.int16),
            pltpu.VMEM((16, BLK + CODE, BLK), jnp.int16),
            dma((2,)), dma((1,)), dma((1,)), dma((2,)), dma((2,)), dma((2,)), dma((2,)),
            dma((12,)), dma((12,)), dma((8, TILES)), dma((8, TILES)), dma((TILES,)), dma((TILES,)),
            dma((TILES,)), dma((TILES,)), dma((TILES,)), dma((TILES,)),
            dma((16,)), dma((16,)),
        ],
        compiler_params=pltpu.CompilerParams(
            collective_id=0, has_side_effects=True, vmem_limit_bytes=56 * 1024 * 1024
        ),
        cost_estimate=pl.CostEstimate(flops=15_000_000_000, bytes_accessed=20_000_000, transcendentals=0),
    )(selected_inverse, pattern, ltil, diag_inverse)


def solution(mesh):
    placed = (P("row", "col"), P("row", "col"), P("row", "col"), P("row", "col"))
    return jax.shard_map(
        local,
        mesh=mesh,
        in_specs=placed,
        out_specs=(P("row", "col"), P("row", "col")),
        check_vma=False,
    )
```

```python
import jax
import jax.numpy as jnp
from jax import lax
from jax.experimental import pallas as pl
from jax.experimental.pallas import tpu as pltpu
from jax.sharding import PartitionSpec as P

MESH = pl.DeviceIdType.MESH
BLK = 128
ROWS = 2560
HALF = 1280
CODE = 16
TILE = 640
TILES = 4
LAST = ROWS - (TILES - 1) * TILE
PACKED = ROWS + TILES * CODE
LATE = [(1, 1), (2, 1)]
F32 = jnp.float32
BF16 = jnp.bfloat16


def device(r, c, k):
    return (r, c * 2 + k)


def xor(a, b, bits):
    out = 0
    for i in range(bits):
        w = 1 << i
        out = out + w * (((a // w) + (b // w)) % 2)
    return out


def swizzle(c):
    return (c // 4) * 4 + ((c // 2 + c // 4) % 2) * 2 + c % 2


def code_of(most):
    return jnp.clip(jnp.floor(jnp.log2(32000.0 / most)), -120.0, 120.0)


def as_int16(values):
    return values.astype(jnp.int32).astype(jnp.int16)


def as_float(values):
    return values.astype(jnp.int32).astype(F32)


def size_of(t):
    return LAST if isinstance(t, int) and t == TILES - 1 else TILE


def span_of(t, step, size):
    return pl.ds(t * step if isinstance(t, int) else pl.multiple_of(t * step, CODE), size)


def rows_of(t):
    return span_of(t, TILE, size_of(t))


def with_code(t):
    return span_of(t, TILE + CODE, size_of(t) + CODE)


def unit_of(code):
    return jnp.exp2(-as_float(code)[0:1, :])


def kernel(
    a_ref, pat_ref, lt_ref, diag_ref,
    panel_ref, corner_ref,
    pat, a_all, b_all, b_turned, total, z_out, z_in, y_out, y_in, slabs, corner, part, parts_in,
    a_sem, core_send, core_recv, first_send, first_recv, pair_send, pair_recv,
    x_send, x_recv, z_send, z_recv, y_send, y_recv,
    slab_send, slab_recv, share_send, share_recv, part_send, part_recv,
):
    r = lax.axis_index("row")
    col = lax.axis_index("col")
    c, k = col // 2, col % 2
    x, yh = r // 2, r % 2
    yl, z = c // 4, c % 4
    home = xor(r, swizzle(c), 3)
    slab = swizzle(xor(r, c, 3))
    x_of = {0: x, 1: (x + 3) % 4, 2: (x + 1) % 4, 3: (x + 2) % 4}
    x_ahead = device(x_of[2] * 2 + yh, c, k)
    x_back = device(x_of[1] * 2 + yh, c, k)
    partner = device(x * 2 + 1 - yh, c, k)
    other = device(r, c, 1 - k)

    barrier = pltpu.get_barrier_semaphore()
    senders = [device(c, swizzle(xor(r, c, 3)), k), other, partner, x_ahead, x_back]
    for i in range(1, 8):
        senders.append(device(r, ((yl + i // 4) % 2) * 4 + xor(z, i % 4, 2), k))
    for b in range(8):
        for kk in range(2):
            senders.append(device(xor(swizzle(c), b, 3), b, kk))
    for s in senders:
        pl.semaphore_signal(barrier, inc=1, device_id=s, device_id_type=MESH)

    own_a = pltpu.make_async_copy(a_ref, a_all.at[k], a_sem.at[0])
    own_a.start()
    own_pat = pltpu.make_async_copy(pat_ref, pat, a_sem.at[1])
    own_pat.start()
    pl.semaphore_wait(barrier, len(senders))

    def remote(src, dst, send, recv, to):
        return pltpu.make_async_remote_copy(
            src_ref=src, dst_ref=dst, send_sem=send, recv_sem=recv, device_id=to, device_id_type=MESH
        )

    stays = jnp.logical_and(r == 0, c == 0)
    halves = [pl.ds(q * HALF, HALF) for q in range(2)]
    first = [
        remote(lt_ref.at[rows], b_all.at[0, rows], first_send.at[q], first_recv.at[q], device(home, r, k))
        for q, rows in enumerate(halves)
    ]

    @pl.when(jnp.logical_not(stays))
    def _():
        for copy in first:
            copy.start()

    @pl.when(stays)
    def _():
        for q, rows in enumerate(halves):
            pltpu.make_async_copy(lt_ref.at[rows], b_all.at[0, rows], first_recv.at[q]).start()

    own_a.wait()
    own_pat.wait()

    def mask(i, carry):
        rows = pl.ds(pl.multiple_of(i * BLK, BLK), BLK)
        for j in range(HALF // BLK):
            keep = jnp.full((BLK, BLK), pat[j, i].astype(F32), F32).astype(BF16)
            cols = slice(j * BLK, (j + 1) * BLK)
            a_all[k, rows, cols] = a_all[k, rows, cols] * keep
        return carry

    lax.fori_loop(0, ROWS // BLK, mask, 0)
    swap = remote(a_all.at[k], a_all.at[k], core_send.at[0], core_recv.at[0], other)
    swap.start()

    def piece(s, q):
        return b_all.at[s, pl.ds(q * HALF, HALF)]

    def along(d, h, q):
        if (d, h) == (3, 1):
            source, to = 6, partner
        else:
            source = {1: h, 2: h, 3: 2 if q == 0 else 4}[d]
            to = x_ahead if d == 1 or (d == 3 and q == 0) else x_back
        i = (d - 1) * 4 + h * 2 + q
        return remote(piece(source, q), piece(2 * d + h, q), x_send.at[i], x_recv.at[i], to)

    def spread(h, q):
        along(1, h, q).start()
        along(2, h, q).start()

    pair = [remote(piece(0, q), piece(1, q), pair_send.at[q], pair_recv.at[q], partner) for q in range(2)]
    for q in range(2):
        first[q].wait_recv()
        spread(0, q)
        pair[q].start()

    remote(a_all.at[1 - k], a_all.at[1 - k], core_send.at[0], core_recv.at[0], other).wait_recv()

    def relation(d, h):
        hi, lo = x_of[d] // 2, x_of[d] % 2
        return hi, ((hi + lo + yl) % 2) * 2 + (yh + h) % 2

    merged = yh == 0
    late_z = [
        jnp.where(x_of[1] // 2 == across, relation(1, 1)[1], relation(2, 1)[1]) for across in range(2)
    ]

    def z_copy(i, t):
        by = i % 4
        if isinstance(i, int):
            hop = by if by != 2 else jnp.where(merged, xor(late_z[i // 4], 2, 2), 2)
        else:
            hop = jnp.where(
                jnp.logical_and(by == 2, merged), xor(jnp.where(i // 4 == 0, late_z[0], late_z[1]), 2, 2), by
            )
        return remote(
            z_out.at[i, with_code(t)], z_in.at[i, with_code(t)], z_send.at[i, t], z_recv.at[i, t],
            device(r, yl * 4 + xor(z, hop, 2), k),
        )

    def y_copy(t):
        return remote(y_out.at[with_code(t)], y_in.at[with_code(t)], y_send.at[t], y_recv.at[t], device(r, (1 - yl) * 4 + z, k))

    def each_tile(body):
        def run(t, carry):
            body(t)
            return carry

        lax.fori_loop(0, TILES, run, 0)


    def packed(values):
        power = code_of(jnp.max(jnp.abs(values), axis=0, keepdims=True))
        code = as_int16(jnp.broadcast_to(power, (CODE, values.shape[1])))
        return as_int16(values * jnp.exp2(power)), code

    def put(ref, t, scaled, code):
        ref[with_code(t), :] = jnp.concatenate([scaled, code], axis=0)

    def unpacked(ref, t):
        ref = ref.at[with_code(t)]
        return as_float(ref[0:size_of(t), :]), unit_of(ref[size_of(t):, :])

    def step(*groups):
        def multiply(t):
            for slots in groups:
                multiply_group(t, slots)

        def multiply_group(t, slots):
            rows = rows_of(t)
            right = [
                jnp.concatenate([b_all[2 * d + h, s, :] for d, h in slots], axis=1)
                for s in (slice(0, HALF), slice(HALF, ROWS))
            ]
            out = jnp.dot(a_all[0, rows, :], right[0], preferred_element_type=F32)
            out = out + jnp.dot(a_all[1, rows, :], right[1], preferred_element_type=F32)
            if slots == LATE:
                held = total.at[0:size_of(t)]
                held[...] = out

                @pl.when(merged)
                def _():
                    for i, slot in enumerate(slots):
                        at = relation(*slot)[0] * 4 + 2
                        cols = slice(i * BLK, (i + 1) * BLK)
                        z_copy(at, t).wait_recv()
                        values, unit = unpacked(z_in.at[at], t)
                        held[:, cols] = held[:, cols] + values * unit

                out = held[...]
            scaled, code = packed(out)
            for i, slot in enumerate(slots):
                across, by = relation(*slot)
                at = across * 4 + by
                cols = slice(i * BLK, (i + 1) * BLK)
                put(z_out.at[at], t, scaled[:, cols], code[:, cols])
                @pl.when(by != 0)
                def _(at=at):
                    z_copy(at, t).start()

        each_tile(multiply)

    def turn(slots):
        for d, h in slots:
            s = 2 * d + h
            for t in range(TILES):
                b_turned[t, s * BLK:(s + 1) * BLK, 0:size_of(t)] = b_all[s, rows_of(t), :].T

    step([(0, 0)])
    along(1, 0, 0).wait_recv()
    along(3, 0, 0).start()
    pair[0].wait_recv()
    spread(1, 0)
    along(2, 0, 1).wait_recv()
    along(3, 0, 1).start()
    pair[1].wait_recv()
    spread(1, 1)
    step([(0, 1)])
    along(1, 0, 1).wait_recv()
    along(2, 0, 0).wait_recv()
    step([(1, 0), (2, 0)])
    for q in range(2):
        along(3, 0, q).wait_recv()
        along(3, 1, q).start()
    step([(3, 0)])
    turn([(0, 0), (0, 1), (1, 0), (2, 0), (3, 0)])
    for d in (1, 2):
        for q in range(2):
            along(d, 1, q).wait_recv()
    for q in range(2):
        along(3, 1, q).wait_recv()
    turn([(1, 1), (2, 1), (3, 1)])
    step(LATE, [(3, 1)])

    def parts_of(across):
        return [z_out.at[across * 4]] + [z_in.at[across * 4 + i] for i in range(1, 4)]

    def sum_of(refs, t):
        out = 0.0
        for i, ref in enumerate(refs):
            values, unit = unpacked(ref, t)
            if i == 2:
                unit = jnp.where(merged, 0.0, unit)
            out = out + values * unit
        return out

    def z_wait(across, t):
        for i in (1, 3):
            z_copy(across * 4 + i, t).wait_recv()

        @pl.when(jnp.logical_not(merged))
        def _():
            z_copy(across * 4 + 2, t).wait_recv()

    def pass_on(t):
        z_wait(1, t)

        put(y_out, t, *packed(sum_of(parts_of(1), t)))
        y_copy(t).start()

    def third(t):
        rows = rows_of(t)
        return remote(panel_ref.at[rows], slabs.at[k, rows], slab_send.at[t], slab_recv.at[t], device(home, r, k))

    def finish(t):
        z_wait(0, t)

        y_copy(t).wait_recv()
        rows = rows_of(t)
        out = sum_of(parts_of(0) + [y_in], t)
        panel_ref[rows, :] = (-out).astype(BF16)

        @pl.when(jnp.logical_not(stays))
        def _():
            third(t).start()

        @pl.when(stays)
        def _():
            pltpu.make_async_copy(panel_ref.at[rows], slabs.at[k, rows], slab_recv.at[t]).start()

    for t in range(TILES + 1):
        if t < TILES:
            pass_on(t)
        if t > 0:
            finish(t - 1)

    def share(t, owner):
        rows = rows_of(t)
        return remote(slabs.at[owner, rows], slabs.at[owner, rows], share_send.at[t], share_recv.at[t], other)

    for t in range(TILES + 1):
        if t < TILES:
            third(t).wait_recv()
            share(t, k).start()
        if t > 0:
            share(t - 1, 1 - k).wait_recv()
            rows = rows_of(t - 1)
            right = jnp.concatenate([slabs[0, rows, :], slabs[1, rows, :]], axis=1)
            for j in range(4):
                span = slice(j * 2 * BLK, (j + 1) * 2 * BLK)
                out = jnp.dot(b_turned[t - 1, span, 0:size_of(t - 1)], right, preferred_element_type=F32)
                corner[span, :] = out if t == 1 else corner[span, :] + out

    def corner_of(j, kk):
        d, h = j // 2, j % 2
        to = swizzle(xor(x_of[d] * 2 + (yh + h) % 2, c, 3))
        own = jnp.logical_and(jnp.logical_and(to == r, slab == c), k == kk)
        i = j * 2 + kk
        copy = remote(
            part.at[i], parts_in.at[c * 2 + k], part_send.at[i], part_recv.at[c * 2 + k], device(to, slab, kk)
        )
        return i, own, copy

    for j in range(8):
        scaled, code = packed(corner[j * BLK:(j + 1) * BLK, :])
        for kk in range(2):
            i, own, copy = corner_of(j, kk)
            part[i, 0:BLK, :] = scaled[:, kk * BLK:(kk + 1) * BLK]
            part[i, BLK:, :] = code[:, kk * BLK:(kk + 1) * BLK]

            @pl.when(own)
            def _(i=i):
                parts_in[c * 2 + k] = part[i]

            @pl.when(jnp.logical_not(own))
            def _(copy=copy):
                copy.start()

    for kk in range(2):
        rows = slice(kk * BLK, (kk + 1) * BLK)
        out = diag_ref[rows, :]
        for b in range(8):
            i = b * 2 + kk
            own = jnp.logical_and(jnp.logical_and(xor(swizzle(c), b, 3) == r, c == b), k == kk)

            @pl.when(jnp.logical_not(own))
            def _(i=i):
                remote(part.at[0], parts_in.at[i], part_send.at[0], part_recv.at[i], other).wait_recv()

            out = out - as_float(parts_in[i, 0:BLK, :]) * unit_of(parts_in[i, BLK:, :])
        corner_ref[rows, :] = out

    @pl.when(jnp.logical_not(stays))
    def _():
        for copy in first:
            copy.wait_send()

    swap.wait_send()
    for q in range(2):
        pair[q].wait_send()
        for d in (1, 2, 3):
            for h in range(2):
                along(d, h, q).wait_send()

    def drain(t):
        for i in (1, 2, 3, 5, 6, 7):
            z_copy(i, t).wait_send()


        @pl.when(jnp.logical_not(stays))
        def _():
            third(t).wait_send()

        y_copy(t).wait_send()
        share(t, k).wait_send()

    each_tile(drain)
    for j in range(8):
        for kk in range(2):
            _, own, copy = corner_of(j, kk)

            @pl.when(jnp.logical_not(own))
            def _(copy=copy):
                copy.wait_send()


def hand_back(panel_ref, corner_ref, panel_out, corner_out):
    panel_out[...] = panel_ref[...]
    corner_out[...] = corner_ref[...]


def local(selected_inverse, pattern, ltil, diag_inverse):
    dma = pltpu.SemaphoreType.DMA
    vmem, anywhere = pl.BlockSpec(memory_space=pltpu.VMEM), pl.BlockSpec(memory_space=pl.ANY)
    panel, corner = pl.pallas_call(
        kernel,
        out_shape=(
            jax.ShapeDtypeStruct((ROWS, BLK), BF16),
            jax.ShapeDtypeStruct((2 * BLK, BLK), F32),
        ),
        in_specs=[anywhere, anywhere, anywhere, vmem],
        out_specs=(vmem, vmem),
        scratch_shapes=[
            pltpu.SMEM((HALF // BLK, ROWS // BLK), jnp.int32),
            pltpu.VMEM((2, ROWS, HALF), BF16),
            pltpu.VMEM((8, ROWS, BLK), BF16),
            pltpu.VMEM((TILES, 8 * BLK, TILE), BF16),
            pltpu.VMEM((TILE, 2 * BLK), F32),
            pltpu.VMEM((8, PACKED, BLK), jnp.int16),
            pltpu.VMEM((8, PACKED, BLK), jnp.int16),
            pltpu.VMEM((PACKED, BLK), jnp.int16),
            pltpu.VMEM((PACKED, BLK), jnp.int16),
            pltpu.VMEM((2, ROWS, BLK), BF16),
            pltpu.VMEM((8 * BLK, 2 * BLK), F32),
            pltpu.VMEM((16, BLK + CODE, BLK), jnp.int16),
            pltpu.VMEM((16, BLK + CODE, BLK), jnp.int16),
            dma((2,)), dma((1,)), dma((1,)), dma((2,)), dma((2,)), dma((2,)), dma((2,)),
            dma((12,)), dma((12,)), dma((8, TILES)), dma((8, TILES)), dma((TILES,)), dma((TILES,)),
            dma((TILES,)), dma((TILES,)), dma((TILES,)), dma((TILES,)),
            dma((16,)), dma((16,)),
        ],
        compiler_params=pltpu.CompilerParams(
            collective_id=0, has_side_effects=True, vmem_limit_bytes=56 * 1024 * 1024
        ),
        cost_estimate=pl.CostEstimate(flops=15_000_000_000, bytes_accessed=20_000_000, transcendentals=0),
    )(selected_inverse, pattern.T, ltil, diag_inverse)
    return pl.pallas_call(
        hand_back,
        out_shape=(
            jax.ShapeDtypeStruct((ROWS, BLK), BF16),
            jax.ShapeDtypeStruct((2 * BLK, BLK), F32),
        ),
        in_specs=[vmem, vmem],
        out_specs=(vmem, vmem),
    )(panel, corner)


def solution(mesh):
    placed = (P("row", "col"), P("row", "col"), P("row", "col"), P("row", "col"))
    return jax.shard_map(
        local,
        mesh=mesh,
        in_specs=placed,
        out_specs=(P("row", "col"), P("row", "col")),
        check_vma=False,
    )
```

```python
import jax
import jax.numpy as jnp
from jax import lax
from jax.experimental import pallas as pl
from jax.experimental.pallas import tpu as pltpu
from jax.sharding import PartitionSpec as P

MESH = pl.DeviceIdType.MESH
BLK = 128
ROWS = 2560
HALF = 1280
CODE = 16
TILE = 640
TILES = 4
LAST = ROWS - (TILES - 1) * TILE
PACKED = ROWS + TILES * CODE
LATE = [(1, 1), (2, 1)]
F32 = jnp.float32
BF16 = jnp.bfloat16


def device(r, c, k):
    return (r, c * 2 + k)


def xor(a, b, bits):
    out = 0
    for i in range(bits):
        w = 1 << i
        out = out + w * (((a // w) + (b // w)) % 2)
    return out


def swizzle(c):
    return (c // 4) * 4 + ((c // 2 + c // 4) % 2) * 2 + c % 2


def code_of(most):
    return jnp.clip(jnp.floor(jnp.log2(32000.0 / most)), -120.0, 120.0)


def as_int16(values):
    return values.astype(jnp.int32).astype(jnp.int16)


def as_float(values):
    return values.astype(jnp.int32).astype(F32)


def size_of(t):
    return LAST if isinstance(t, int) and t == TILES - 1 else TILE


def span_of(t, step, size):
    return pl.ds(t * step if isinstance(t, int) else pl.multiple_of(t * step, CODE), size)


def rows_of(t):
    return span_of(t, TILE, size_of(t))


def with_code(t):
    return span_of(t, TILE + CODE, size_of(t) + CODE)


def unit_of(code):
    return jnp.exp2(-as_float(code)[0:1, :])


def kernel(
    a_ref, pat_ref, lt_ref, diag_ref,
    panel_ref, corner_ref,
    pat, a_all, b_all, b_turned, total, z_out, z_in, y_out, y_in, slabs, corner, part, parts_in,
    a_sem, core_send, core_recv, first_send, first_recv, pair_send, pair_recv,
    x_send, x_recv, z_send, z_recv, y_send, y_recv,
    slab_send, slab_recv, turn_send, turn_recv, part_send, part_recv,
):
    r = lax.axis_index("row")
    col = lax.axis_index("col")
    c, k = col // 2, col % 2
    x, yh = r // 2, r % 2
    yl, z = c // 4, c % 4
    home = xor(r, swizzle(c), 3)
    slab = swizzle(xor(r, c, 3))
    x_of = {0: x, 1: (x + 3) % 4, 2: (x + 1) % 4, 3: (x + 2) % 4}
    x_ahead = device(x_of[2] * 2 + yh, c, k)
    x_back = device(x_of[1] * 2 + yh, c, k)
    partner = device(x * 2 + 1 - yh, c, k)
    other = device(r, c, 1 - k)

    barrier = pltpu.get_barrier_semaphore()
    senders = [device(c, swizzle(xor(r, c, 3)), k), other, partner, x_ahead, x_back]
    for i in range(1, 8):
        senders.append(device(r, ((yl + i // 4) % 2) * 4 + xor(z, i % 4, 2), k))
    for b in range(8):
        senders.append(device(xor(swizzle(c), b, 3), b, k))
    for s in senders:
        pl.semaphore_signal(barrier, inc=1, device_id=s, device_id_type=MESH)

    own_a = pltpu.make_async_copy(a_ref, a_all.at[k], a_sem.at[0])
    own_a.start()
    own_pat = pltpu.make_async_copy(pat_ref, pat, a_sem.at[1])
    own_pat.start()
    pl.semaphore_wait(barrier, len(senders))

    def remote(src, dst, send, recv, to):
        return pltpu.make_async_remote_copy(
            src_ref=src, dst_ref=dst, send_sem=send, recv_sem=recv, device_id=to, device_id_type=MESH
        )

    stays = jnp.logical_and(r == 0, c == 0)
    halves = [pl.ds(q * HALF, HALF) for q in range(2)]
    first = [
        remote(lt_ref.at[rows], b_all.at[0, rows], first_send.at[q], first_recv.at[q], device(home, r, k))
        for q, rows in enumerate(halves)
    ]

    @pl.when(jnp.logical_not(stays))
    def _():
        for copy in first:
            copy.start()

    @pl.when(stays)
    def _():
        for q, rows in enumerate(halves):
            pltpu.make_async_copy(lt_ref.at[rows], b_all.at[0, rows], first_recv.at[q]).start()

    own_a.wait()
    own_pat.wait()

    def mask(i, carry):
        rows = pl.ds(pl.multiple_of(i * BLK, BLK), BLK)
        for j in range(HALF // BLK):
            keep = jnp.full((BLK, BLK), pat[j, i].astype(F32), F32).astype(BF16)
            cols = slice(j * BLK, (j + 1) * BLK)
            a_all[k, rows, cols] = a_all[k, rows, cols] * keep
        return carry

    lax.fori_loop(0, ROWS // BLK, mask, 0)
    swap = remote(a_all.at[k], a_all.at[k], core_send.at[0], core_recv.at[0], other)
    swap.start()

    def piece(s, q):
        return b_all.at[s, pl.ds(q * HALF, HALF)]

    def along(d, h, q):
        if (d, h) == (3, 1):
            source, to = 6, partner
        else:
            source = {1: h, 2: h, 3: 2 if q == 0 else 4}[d]
            to = x_ahead if d == 1 or (d == 3 and q == 0) else x_back
        i = (d - 1) * 4 + h * 2 + q
        return remote(piece(source, q), piece(2 * d + h, q), x_send.at[i], x_recv.at[i], to)

    def spread(h, q):
        along(1, h, q).start()
        along(2, h, q).start()

    pair = [remote(piece(0, q), piece(1, q), pair_send.at[q], pair_recv.at[q], partner) for q in range(2)]
    for q in range(2):
        first[q].wait_recv()
        spread(0, q)
        pair[q].start()

    remote(a_all.at[1 - k], a_all.at[1 - k], core_send.at[0], core_recv.at[0], other).wait_recv()

    def relation(d, h):
        hi, lo = x_of[d] // 2, x_of[d] % 2
        return hi, ((hi + lo + yl) % 2) * 2 + (yh + h) % 2

    merged = yh == 0
    late_z = [
        jnp.where(x_of[1] // 2 == across, relation(1, 1)[1], relation(2, 1)[1]) for across in range(2)
    ]

    def z_copy(i, t):
        by = i % 4
        if isinstance(i, int):
            hop = by if by != 2 else jnp.where(merged, xor(late_z[i // 4], 2, 2), 2)
        else:
            hop = jnp.where(
                jnp.logical_and(by == 2, merged), xor(jnp.where(i // 4 == 0, late_z[0], late_z[1]), 2, 2), by
            )
        return remote(
            z_out.at[i, with_code(t)], z_in.at[i, with_code(t)], z_send.at[i, t], z_recv.at[i, t],
            device(r, yl * 4 + xor(z, hop, 2), k),
        )

    def y_copy(t):
        return remote(y_out.at[with_code(t)], y_in.at[with_code(t)], y_send.at[t], y_recv.at[t], device(r, (1 - yl) * 4 + z, k))

    def each_tile(body):
        def run(t, carry):
            body(t)
            return carry

        lax.fori_loop(0, TILES, run, 0)


    def packed(values):
        power = code_of(jnp.max(jnp.abs(values), axis=0, keepdims=True))
        code = as_int16(jnp.broadcast_to(power, (CODE, values.shape[1])))
        return as_int16(values * jnp.exp2(power)), code

    def put(ref, t, scaled, code):
        ref[with_code(t), :] = jnp.concatenate([scaled, code], axis=0)

    def unpacked(ref, t):
        ref = ref.at[with_code(t)]
        return as_float(ref[0:size_of(t), :]), unit_of(ref[size_of(t):, :])

    def step(*groups):
        def multiply(t):
            for slots in groups:
                multiply_group(t, slots)

        def multiply_group(t, slots):
            rows = rows_of(t)
            right = [
                jnp.concatenate([b_all[2 * d + h, s, :] for d, h in slots], axis=1)
                for s in (slice(0, HALF), slice(HALF, ROWS))
            ]
            out = jnp.dot(a_all[0, rows, :], right[0], preferred_element_type=F32)
            out = out + jnp.dot(a_all[1, rows, :], right[1], preferred_element_type=F32)
            if slots == LATE:
                held = total.at[0:size_of(t)]
                held[...] = out

                @pl.when(merged)
                def _():
                    for i, slot in enumerate(slots):
                        at = relation(*slot)[0] * 4 + 2
                        cols = slice(i * BLK, (i + 1) * BLK)
                        z_copy(at, t).wait_recv()
                        values, unit = unpacked(z_in.at[at], t)
                        held[:, cols] = held[:, cols] + values * unit

                out = held[...]
            scaled, code = packed(out)
            for i, slot in enumerate(slots):
                across, by = relation(*slot)
                at = across * 4 + by
                cols = slice(i * BLK, (i + 1) * BLK)
                put(z_out.at[at], t, scaled[:, cols], code[:, cols])
                @pl.when(by != 0)
                def _(at=at):
                    z_copy(at, t).start()

        each_tile(multiply)

    def turned(s, owner):
        part_of = b_turned.at[owner, :, pl.ds(s * BLK, BLK)]
        return remote(part_of, part_of, turn_send.at[s], turn_recv.at[s], other)

    def turn(slots):
        for d, h in slots:
            s = 2 * d + h
            for t in range(TILES):
                b_turned[k, t, s * BLK:(s + 1) * BLK, :] = b_all[s, rows_of(t), :].T
            turned(s, k).start()

    step([(0, 0)])
    along(1, 0, 0).wait_recv()
    along(3, 0, 0).start()
    pair[0].wait_recv()
    spread(1, 0)
    along(2, 0, 1).wait_recv()
    along(3, 0, 1).start()
    pair[1].wait_recv()
    spread(1, 1)
    step([(0, 1)])
    along(1, 0, 1).wait_recv()
    along(2, 0, 0).wait_recv()
    step([(1, 0), (2, 0)])
    for q in range(2):
        along(3, 0, q).wait_recv()
        along(3, 1, q).start()
    step([(3, 0)])
    turn([(0, 0), (0, 1), (1, 0), (2, 0), (3, 0)])
    for d in (1, 2):
        for q in range(2):
            along(d, 1, q).wait_recv()
    for q in range(2):
        along(3, 1, q).wait_recv()
    turn([(1, 1), (2, 1), (3, 1)])
    step(LATE, [(3, 1)])

    def parts_of(across):
        return [z_out.at[across * 4]] + [z_in.at[across * 4 + i] for i in range(1, 4)]

    def sum_of(refs, t):
        out = 0.0
        for i, ref in enumerate(refs):
            values, unit = unpacked(ref, t)
            if i == 2:
                unit = jnp.where(merged, 0.0, unit)
            out = out + values * unit
        return out

    def z_wait(across, t):
        for i in (1, 3):
            z_copy(across * 4 + i, t).wait_recv()

        @pl.when(jnp.logical_not(merged))
        def _():
            z_copy(across * 4 + 2, t).wait_recv()

    def pass_on(t):
        z_wait(1, t)

        put(y_out, t, *packed(sum_of(parts_of(1), t)))
        y_copy(t).start()

    def third(t):
        rows = rows_of(t)
        return remote(panel_ref.at[rows], slabs.at[rows], slab_send.at[t], slab_recv.at[t], device(home, r, k))

    def finish(t):
        z_wait(0, t)

        y_copy(t).wait_recv()
        rows = rows_of(t)
        out = sum_of(parts_of(0) + [y_in], t)
        panel_ref[rows, :] = (-out).astype(BF16)

        @pl.when(jnp.logical_not(stays))
        def _():
            third(t).start()

        @pl.when(stays)
        def _():
            pltpu.make_async_copy(panel_ref.at[rows], slabs.at[rows], slab_recv.at[t]).start()

    for t in range(TILES + 1):
        if t < TILES:
            pass_on(t)
        if t > 0:
            finish(t - 1)

    for s in range(8):
        turned(s, 1 - k).wait_recv()
    for t in range(TILES):
        third(t).wait_recv()
        right = slabs[rows_of(t), :]
        for kk in range(2):
            for j in range(4):
                span = slice(j * 2 * BLK, (j + 1) * 2 * BLK)
                out = jnp.dot(b_turned[kk, t, span, :], right, preferred_element_type=F32)
                corner[kk, span, :] = out if t == 0 else corner[kk, span, :] + out

    def corner_of(j):
        to = swizzle(xor(x_of[j // 2] * 2 + (yh + j % 2) % 2, c, 3))
        own = jnp.logical_and(to == r, slab == c)
        return own, remote(part.at[j], parts_in.at[c], part_send.at[j], part_recv.at[c], device(to, slab, k))

    for j in range(8):
        span = slice(j * BLK, (j + 1) * BLK)
        scaled, code = packed(jnp.concatenate([corner[0, span, :], corner[1, span, :]], axis=0))
        part[j] = jnp.concatenate([scaled, code], axis=0)
        own, copy = corner_of(j)

        @pl.when(own)
        def _(j=j):
            parts_in[c] = part[j]

        @pl.when(jnp.logical_not(own))
        def _(copy=copy):
            copy.start()

    out = diag_ref[...]
    for b in range(8):
        own = jnp.logical_and(xor(swizzle(c), b, 3) == r, c == b)

        @pl.when(jnp.logical_not(own))
        def _(b=b):
            remote(part.at[0], parts_in.at[b], part_send.at[0], part_recv.at[b], other).wait_recv()

        out = out - as_float(parts_in[b, 0:2 * BLK, :]) * unit_of(parts_in[b, 2 * BLK:, :])
    corner_ref[...] = out

    @pl.when(jnp.logical_not(stays))
    def _():
        for copy in first:
            copy.wait_send()

    swap.wait_send()
    for q in range(2):
        pair[q].wait_send()
        for d in (1, 2, 3):
            for h in range(2):
                along(d, h, q).wait_send()

    def drain(t):
        for i in (1, 2, 3, 5, 6, 7):
            z_copy(i, t).wait_send()


        @pl.when(jnp.logical_not(stays))
        def _():
            third(t).wait_send()

        y_copy(t).wait_send()

    each_tile(drain)
    for j in range(8):
        turned(j, k).wait_send()
        own, copy = corner_of(j)

        @pl.when(jnp.logical_not(own))
        def _(copy=copy):
            copy.wait_send()


def hand_back(panel_ref, corner_ref, panel_out, corner_out):
    panel_out[...] = panel_ref[...]
    corner_out[...] = corner_ref[...]


def local(selected_inverse, pattern, ltil, diag_inverse):
    dma = pltpu.SemaphoreType.DMA
    vmem, anywhere = pl.BlockSpec(memory_space=pltpu.VMEM), pl.BlockSpec(memory_space=pl.ANY)
    panel, corner = pl.pallas_call(
        kernel,
        out_shape=(
            jax.ShapeDtypeStruct((ROWS, BLK), BF16),
            jax.ShapeDtypeStruct((2 * BLK, BLK), F32),
        ),
        in_specs=[anywhere, anywhere, anywhere, vmem],
        out_specs=(vmem, vmem),
        scratch_shapes=[
            pltpu.SMEM((HALF // BLK, ROWS // BLK), jnp.int32),
            pltpu.VMEM((2, ROWS, HALF), BF16),
            pltpu.VMEM((8, ROWS, BLK), BF16),
            pltpu.VMEM((2, TILES, 8 * BLK, TILE), BF16),
            pltpu.VMEM((TILE, 2 * BLK), F32),
            pltpu.VMEM((8, PACKED, BLK), jnp.int16),
            pltpu.VMEM((8, PACKED, BLK), jnp.int16),
            pltpu.VMEM((PACKED, BLK), jnp.int16),
            pltpu.VMEM((PACKED, BLK), jnp.int16),
            pltpu.VMEM((ROWS, BLK), BF16),
            pltpu.VMEM((2, 8 * BLK, BLK), F32),
            pltpu.VMEM((8, 2 * BLK + CODE, BLK), jnp.int16),
            pltpu.VMEM((8, 2 * BLK + CODE, BLK), jnp.int16),
            dma((2,)), dma((1,)), dma((1,)), dma((2,)), dma((2,)), dma((2,)), dma((2,)),
            dma((12,)), dma((12,)), dma((8, TILES)), dma((8, TILES)), dma((TILES,)), dma((TILES,)),
            dma((TILES,)), dma((TILES,)), dma((8,)), dma((8,)),
            dma((8,)), dma((8,)),
        ],
        compiler_params=pltpu.CompilerParams(
            collective_id=0, has_side_effects=True, vmem_limit_bytes=56 * 1024 * 1024
        ),
        cost_estimate=pl.CostEstimate(flops=15_000_000_000, bytes_accessed=20_000_000, transcendentals=0),
    )(selected_inverse, pattern.T, ltil, diag_inverse)
    return pl.pallas_call(
        hand_back,
        out_shape=(
            jax.ShapeDtypeStruct((ROWS, BLK), BF16),
            jax.ShapeDtypeStruct((2 * BLK, BLK), F32),
        ),
        in_specs=[vmem, vmem],
        out_specs=(vmem, vmem),
    )(panel, corner)


def solution(mesh):
    placed = (P("row", "col"), P("row", "col"), P("row", "col"), P("row", "col"))
    return jax.shard_map(
        local,
        mesh=mesh,
        in_specs=placed,
        out_specs=(P("row", "col"), P("row", "col")),
        check_vma=False,
    )
```

```python
import jax
import jax.numpy as jnp
from jax import lax
from jax.experimental import pallas as pl
from jax.experimental.pallas import tpu as pltpu
from jax.sharding import PartitionSpec as P

MESH = pl.DeviceIdType.MESH
BLK = 128
ROWS = 2560
HALF = 1280
CODE = 16
TILE = 640
TILES = 4
LAST = ROWS - (TILES - 1) * TILE
PACKED = ROWS + TILES * CODE
LATE = [(1, 1), (2, 1)]
EARLY = [(3, 0)]
KEPT = 2
F32 = jnp.float32
BF16 = jnp.bfloat16


def device(r, c, k):
    return (r, c * 2 + k)


def xor(a, b, bits):
    out = 0
    for i in range(bits):
        w = 1 << i
        out = out + w * (((a // w) + (b // w)) % 2)
    return out


def swizzle(c):
    return (c // 4) * 4 + ((c // 2 + c // 4) % 2) * 2 + c % 2


def code_of(most):
    return jnp.clip(jnp.floor(jnp.log2(32000.0 / most)), -120.0, 120.0)


def as_int16(values):
    return values.astype(jnp.int32).astype(jnp.int16)


def as_float(values):
    return values.astype(jnp.int32).astype(F32)


def size_of(t):
    return LAST if isinstance(t, int) and t == TILES - 1 else TILE


def span_of(t, step, size):
    return pl.ds(t * step if isinstance(t, int) else pl.multiple_of(t * step, CODE), size)


def rows_of(t):
    return span_of(t, TILE, size_of(t))


def with_code(t):
    return span_of(t, TILE + CODE, size_of(t) + CODE)


def unit_of(code):
    return jnp.exp2(-as_float(code)[0:1, :])


def kernel(
    a_ref, pat_ref, lt_ref, diag_ref,
    panel_ref, corner_ref,
    pat, a_all, b_all, b_turned, total, z_out, z_in, y_out, y_in, mine, slabs, corner, part, parts_in,
    a_sem, core_send, core_recv, first_send, first_recv, pair_send, pair_recv,
    x_send, x_recv, z_send, z_recv, y_send, y_recv,
    slab_send, slab_recv, turn_send, turn_recv, part_send, part_recv,
):
    r = lax.axis_index("row")
    col = lax.axis_index("col")
    c, k = col // 2, col % 2
    x, yh = r // 2, r % 2
    yl, z = c // 4, c % 4
    home = xor(r, swizzle(c), 3)
    slab = swizzle(xor(r, c, 3))
    x_of = {0: x, 1: (x + 3) % 4, 2: (x + 1) % 4, 3: (x + 2) % 4}
    x_ahead = device(x_of[2] * 2 + yh, c, k)
    x_back = device(x_of[1] * 2 + yh, c, k)
    partner = device(x * 2 + 1 - yh, c, k)
    other = device(r, c, 1 - k)

    barrier = pltpu.get_barrier_semaphore()
    senders = [device(c, swizzle(xor(r, c, 3)), k), other, partner, x_ahead, x_back]
    for i in range(1, 8):
        senders.append(device(r, ((yl + i // 4) % 2) * 4 + xor(z, i % 4, 2), k))
    for b in range(8):
        senders.append(device(xor(swizzle(c), b, 3), b, k))
    for s in senders:
        pl.semaphore_signal(barrier, inc=1, device_id=s, device_id_type=MESH)

    own_a = pltpu.make_async_copy(a_ref, a_all.at[k], a_sem.at[0])
    own_a.start()
    own_pat = pltpu.make_async_copy(pat_ref, pat, a_sem.at[1])
    own_pat.start()
    pl.semaphore_wait(barrier, len(senders))

    def remote(src, dst, send, recv, to):
        return pltpu.make_async_remote_copy(
            src_ref=src, dst_ref=dst, send_sem=send, recv_sem=recv, device_id=to, device_id_type=MESH
        )

    stays = jnp.logical_and(r == 0, c == 0)
    halves = [pl.ds(q * HALF, HALF) for q in range(2)]
    first = [
        remote(lt_ref.at[rows], b_all.at[0, rows], first_send.at[q], first_recv.at[q], device(home, r, k))
        for q, rows in enumerate(halves)
    ]

    @pl.when(jnp.logical_not(stays))
    def _():
        for copy in first:
            copy.start()

    @pl.when(stays)
    def _():
        for q, rows in enumerate(halves):
            pltpu.make_async_copy(lt_ref.at[rows], b_all.at[0, rows], first_recv.at[q]).start()

    own_a.wait()
    own_pat.wait()

    def mask(i, carry):
        rows = pl.ds(pl.multiple_of(i * BLK, BLK), BLK)
        for j in range(HALF // BLK):
            keep = jnp.full((BLK, BLK), pat[j, i].astype(F32), F32).astype(BF16)
            cols = slice(j * BLK, (j + 1) * BLK)
            a_all[k, rows, cols] = a_all[k, rows, cols] * keep
        return carry

    lax.fori_loop(0, ROWS // BLK, mask, 0)
    swap = remote(a_all.at[k], a_all.at[k], core_send.at[0], core_recv.at[0], other)
    swap.start()

    def piece(s, q):
        return b_all.at[s, pl.ds(q * HALF, HALF)]

    def along(d, h, q):
        if (d, h) == (3, 1):
            source, to = 6, partner
        else:
            source = {1: h, 2: h, 3: 2 if q == 0 else 4}[d]
            to = x_ahead if d == 1 or (d == 3 and q == 0) else x_back
        i = (d - 1) * 4 + h * 2 + q
        return remote(piece(source, q), piece(2 * d + h, q), x_send.at[i], x_recv.at[i], to)

    def spread(h, q):
        along(1, h, q).start()
        along(2, h, q).start()

    pair = [remote(piece(0, q), piece(1, q), pair_send.at[q], pair_recv.at[q], partner) for q in range(2)]
    for q in range(2):
        first[q].wait_recv()
        spread(0, q)
        pair[q].start()

    remote(a_all.at[1 - k], a_all.at[1 - k], core_send.at[0], core_recv.at[0], other).wait_recv()

    def relation(d, h):
        hi, lo = x_of[d] // 2, x_of[d] % 2
        return hi, ((hi + lo + yl) % 2) * 2 + (yh + h) % 2

    merged = yh == 0
    late_z = [
        jnp.where(x_of[1] // 2 == across, relation(1, 1)[1], relation(2, 1)[1]) for across in range(2)
    ]

    def z_copy(i, t):
        by = i % 4
        if isinstance(i, int):
            hop = by if by != 2 else jnp.where(merged, xor(late_z[i // 4], 2, 2), 2)
        else:
            hop = jnp.where(
                jnp.logical_and(by == 2, merged), xor(jnp.where(i // 4 == 0, late_z[0], late_z[1]), 2, 2), by
            )
        return remote(
            z_out.at[i, with_code(t)], z_in.at[i, with_code(t)], z_send.at[i, t], z_recv.at[i, t],
            device(r, yl * 4 + xor(z, hop, 2), k),
        )

    def y_copy(t):
        return remote(y_out.at[with_code(t)], y_in.at[with_code(t)], y_send.at[t], y_recv.at[t], device(r, (1 - yl) * 4 + z, k))

    def each_tile(body):
        def run(t, carry):
            body(t)
            return carry

        lax.fori_loop(0, TILES, run, 0)


    def packed(values):
        power = code_of(jnp.max(jnp.abs(values), axis=0, keepdims=True))
        code = as_int16(jnp.broadcast_to(power, (CODE, values.shape[1])))
        return as_int16(values * jnp.exp2(power)), code

    def put(ref, t, scaled, code):
        ref[with_code(t), :] = jnp.concatenate([scaled, code], axis=0)

    def unpacked(ref, t):
        ref = ref.at[with_code(t)]
        return as_float(ref[0:size_of(t), :]), unit_of(ref[size_of(t):, :])

    def step(*groups):
        def multiply(t):
            for slots in groups:
                multiply_group(t, slots)

        def multiply_group(t, slots):
            rows = rows_of(t)
            right = [
                jnp.concatenate([b_all[2 * d + h, s, :] for d, h in slots], axis=1)
                for s in (slice(0, HALF), slice(HALF, ROWS))
            ]
            out = jnp.dot(a_all[0, rows, :], right[0], preferred_element_type=F32)
            out = out + jnp.dot(a_all[1, rows, :], right[1], preferred_element_type=F32)
            if slots == LATE:
                held = total.at[0:size_of(t)]
                held[...] = out

                @pl.when(merged)
                def _():
                    for i, slot in enumerate(slots):
                        at = relation(*slot)[0] * 4 + 2
                        cols = slice(i * BLK, (i + 1) * BLK)
                        z_copy(at, t).wait_recv()
                        values, unit = unpacked(z_in.at[at], t)
                        held[:, cols] = held[:, cols] + values * unit

                out = held[...]
            scaled, code = packed(out)
            for i, slot in enumerate(slots):
                across, by = relation(*slot)
                at = across * 4 + by
                cols = slice(i * BLK, (i + 1) * BLK)
                put(z_out.at[at], t, scaled[:, cols], code[:, cols])
                moves = by != 0
                if slot in EARLY:
                    moves = jnp.logical_and(moves, jnp.logical_or(merged, t < KEPT))

                @pl.when(moves)
                def _(at=at):
                    z_copy(at, t).start()

            if (3, 1) in slots:
                for slot in EARLY:
                    across, by = relation(*slot)

                    @pl.when(jnp.logical_and(jnp.logical_and(by != 0, jnp.logical_not(merged)), t < TILES - KEPT))
                    def _(at=across * 4 + by):
                        z_copy(at, t + KEPT).start()

        each_tile(multiply)

    def turned(s, owner):
        part_of = b_turned.at[owner, :, pl.ds(s * BLK, BLK)]
        return remote(part_of, part_of, turn_send.at[s], turn_recv.at[s], other)

    def turn(slots):
        for d, h in slots:
            s = 2 * d + h
            for t in range(TILES):
                b_turned[k, t, s * BLK:(s + 1) * BLK, :] = b_all[s, rows_of(t), :].T
            turned(s, k).start()

    step([(0, 0)])
    along(1, 0, 0).wait_recv()
    along(3, 0, 0).start()
    pair[0].wait_recv()
    spread(1, 0)
    along(2, 0, 1).wait_recv()
    along(3, 0, 1).start()
    pair[1].wait_recv()
    spread(1, 1)
    step([(0, 1)])
    along(1, 0, 1).wait_recv()
    along(2, 0, 0).wait_recv()
    step([(1, 0), (2, 0)])
    for q in range(2):
        along(3, 0, q).wait_recv()
        along(3, 1, q).start()
    step([(3, 0)])
    turn([(0, 0), (0, 1), (1, 0), (2, 0), (3, 0)])
    for d in (1, 2):
        for q in range(2):
            along(d, 1, q).wait_recv()
    turn([(1, 1), (2, 1)])
    for q in range(2):
        along(3, 1, q).wait_recv()
    step(LATE, [(3, 1)])
    turn([(3, 1)])

    def parts_of(across):
        return [z_out.at[across * 4]] + [z_in.at[across * 4 + i] for i in range(1, 4)]

    def sum_of(refs, t):
        out = 0.0
        for i, ref in enumerate(refs):
            values, unit = unpacked(ref, t)
            if i == 2:
                unit = jnp.where(merged, 0.0, unit)
            out = out + values * unit
        return out

    def z_wait(across, t):
        for i in (1, 3):
            z_copy(across * 4 + i, t).wait_recv()

        @pl.when(jnp.logical_not(merged))
        def _():
            z_copy(across * 4 + 2, t).wait_recv()

    def pass_on(t):
        z_wait(1, t)

        put(y_out, t, *packed(sum_of(parts_of(1), t)))
        y_copy(t).start()

    def third(t):
        rows = rows_of(t)
        return remote(mine.at[rows], slabs.at[rows], slab_send.at[t], slab_recv.at[t], device(home, r, k))

    def finish(t):
        z_wait(0, t)

        y_copy(t).wait_recv()
        rows = rows_of(t)
        out = sum_of(parts_of(0) + [y_in], t)
        mine[rows, :] = (-out).astype(BF16)
        panel_ref[rows, :] = (-out).astype(BF16)

        @pl.when(jnp.logical_not(stays))
        def _():
            third(t).start()

        @pl.when(stays)
        def _():
            pltpu.make_async_copy(mine.at[rows], slabs.at[rows], slab_recv.at[t]).start()

    for t in range(TILES + 1):
        if t < TILES:
            pass_on(t)
        if t > 0:
            finish(t - 1)

    for s in range(8):
        turned(s, 1 - k).wait_recv()
    for t in range(TILES):
        third(t).wait_recv()
        right = slabs[rows_of(t), :]
        for kk in range(2):
            for j in range(4):
                span = slice(j * 2 * BLK, (j + 1) * 2 * BLK)
                out = jnp.dot(b_turned[kk, t, span, :], right, preferred_element_type=F32)
                corner[kk, span, :] = out if t == 0 else corner[kk, span, :] + out

    def corner_of(j):
        to = swizzle(xor(x_of[j // 2] * 2 + (yh + j % 2) % 2, c, 3))
        own = jnp.logical_and(to == r, slab == c)
        return own, remote(part.at[j], parts_in.at[c], part_send.at[j], part_recv.at[c], device(to, slab, k))

    for j in range(8):
        span = slice(j * BLK, (j + 1) * BLK)
        scaled, code = packed(jnp.concatenate([corner[0, span, :], corner[1, span, :]], axis=0))
        part[j] = jnp.concatenate([scaled, code], axis=0)
        own, copy = corner_of(j)

        @pl.when(own)
        def _(j=j):
            parts_in[c] = part[j]

        @pl.when(jnp.logical_not(own))
        def _(copy=copy):
            copy.start()

    out = diag_ref[...]
    for b in range(8):
        own = jnp.logical_and(xor(swizzle(c), b, 3) == r, c == b)

        @pl.when(jnp.logical_not(own))
        def _(b=b):
            remote(part.at[0], parts_in.at[b], part_send.at[0], part_recv.at[b], other).wait_recv()

        out = out - as_float(parts_in[b, 0:2 * BLK, :]) * unit_of(parts_in[b, 2 * BLK:, :])
    corner_ref[...] = out

    @pl.when(jnp.logical_not(stays))
    def _():
        for copy in first:
            copy.wait_send()

    swap.wait_send()
    for q in range(2):
        pair[q].wait_send()
        for d in (1, 2, 3):
            for h in range(2):
                along(d, h, q).wait_send()

    def drain(t):
        for i in (1, 2, 3, 5, 6, 7):
            z_copy(i, t).wait_send()


        @pl.when(jnp.logical_not(stays))
        def _():
            third(t).wait_send()

        y_copy(t).wait_send()

    each_tile(drain)
    for j in range(8):
        turned(j, k).wait_send()
        own, copy = corner_of(j)

        @pl.when(jnp.logical_not(own))
        def _(copy=copy):
            copy.wait_send()


def hand_back(panel_ref, corner_ref, panel_out, corner_out):
    panel_out[...] = panel_ref[...]
    corner_out[...] = corner_ref[...]


def local(selected_inverse, pattern, ltil, diag_inverse):
    dma = pltpu.SemaphoreType.DMA
    vmem, anywhere = pl.BlockSpec(memory_space=pltpu.VMEM), pl.BlockSpec(memory_space=pl.ANY)
    panel, corner = pl.pallas_call(
        kernel,
        out_shape=(
            jax.ShapeDtypeStruct((ROWS, BLK), BF16),
            jax.ShapeDtypeStruct((2 * BLK, BLK), F32),
        ),
        in_specs=[anywhere, anywhere, anywhere, vmem],
        out_specs=(vmem, vmem),
        scratch_shapes=[
            pltpu.SMEM((HALF // BLK, ROWS // BLK), jnp.int32),
            pltpu.VMEM((2, ROWS, HALF), BF16),
            pltpu.VMEM((8, ROWS, BLK), BF16),
            pltpu.VMEM((2, TILES, 8 * BLK, TILE), BF16),
            pltpu.VMEM((TILE, 2 * BLK), F32),
            pltpu.VMEM((8, PACKED, BLK), jnp.int16),
            pltpu.VMEM((8, PACKED, BLK), jnp.int16),
            pltpu.VMEM((PACKED, BLK), jnp.int16),
            pltpu.VMEM((PACKED, BLK), jnp.int16),
            pltpu.VMEM((ROWS, BLK), BF16),
            pltpu.VMEM((ROWS, BLK), BF16),
            pltpu.VMEM((2, 8 * BLK, BLK), F32),
            pltpu.VMEM((8, 2 * BLK + CODE, BLK), jnp.int16),
            pltpu.VMEM((8, 2 * BLK + CODE, BLK), jnp.int16),
            dma((2,)), dma((1,)), dma((1,)), dma((2,)), dma((2,)), dma((2,)), dma((2,)),
            dma((12,)), dma((12,)), dma((8, TILES)), dma((8, TILES)), dma((TILES,)), dma((TILES,)),
            dma((TILES,)), dma((TILES,)), dma((8,)), dma((8,)),
            dma((8,)), dma((8,)),
        ],
        compiler_params=pltpu.CompilerParams(
            collective_id=0, has_side_effects=True, vmem_limit_bytes=56 * 1024 * 1024
        ),
        cost_estimate=pl.CostEstimate(flops=15_000_000_000, bytes_accessed=20_000_000, transcendentals=0),
    )(selected_inverse, pattern.T, ltil, diag_inverse)
    return pl.pallas_call(
        hand_back,
        out_shape=(
            jax.ShapeDtypeStruct((ROWS, BLK), BF16),
            jax.ShapeDtypeStruct((2 * BLK, BLK), F32),
        ),
        in_specs=[vmem, vmem],
        out_specs=(vmem, vmem),
    )(panel, corner)


def solution(mesh):
    placed = (P("row", "col"), P("row", "col"), P("row", "col"), P("row", "col"))
    return jax.shard_map(
        local,
        mesh=mesh,
        in_specs=placed,
        out_specs=(P("row", "col"), P("row", "col")),
        check_vma=False,
    )
```

```python
import jax
import jax.numpy as jnp
from jax import lax
from jax.experimental import pallas as pl
from jax.experimental.pallas import tpu as pltpu
from jax.sharding import PartitionSpec as P

MESH = pl.DeviceIdType.MESH
BLK = 128
ROWS = 2560
HALF = 1280
CODE = 16
TILE = 640
TILES = 4
LAST = ROWS - (TILES - 1) * TILE
PACKED = ROWS + TILES * CODE
LATE = [(1, 1), (2, 1)]
EARLY = [(3, 0)]
KEPT = 2
F32 = jnp.float32
BF16 = jnp.bfloat16


def device(r, c, k):
    return (r, c * 2 + k)


def xor(a, b, bits):
    out = 0
    for i in range(bits):
        w = 1 << i
        out = out + w * (((a // w) + (b // w)) % 2)
    return out


def swizzle(c):
    return (c // 4) * 4 + ((c // 2 + c // 4) % 2) * 2 + c % 2


def code_of(most):
    return jnp.clip(jnp.floor(jnp.log2(32000.0 / most)), -120.0, 120.0)


def as_int16(values):
    return values.astype(jnp.int32).astype(jnp.int16)


def as_float(values):
    return values.astype(jnp.int32).astype(F32)


def size_of(t):
    return LAST if isinstance(t, int) and t == TILES - 1 else TILE


def span_of(t, step, size):
    return pl.ds(t * step if isinstance(t, int) else pl.multiple_of(t * step, CODE), size)


def rows_of(t):
    return span_of(t, TILE, size_of(t))


def with_code(t):
    return span_of(t, TILE + CODE, size_of(t) + CODE)


def unit_of(code):
    return jnp.exp2(-as_float(code)[0:1, :])


def kernel(
    a_ref, pat_ref, lt_ref, diag_ref,
    panel_ref, corner_ref,
    pat, a_all, b_all, b_turned, total, z_out, z_in, y_out, y_in, mine, slabs, corner, part, parts_in,
    a_sem, core_send, core_recv, first_send, first_recv, pair_send, pair_recv,
    x_send, x_recv, z_send, z_recv, y_send, y_recv,
    slab_send, slab_recv, turn_send, turn_recv, part_send, part_recv,
):
    r = lax.axis_index("row")
    col = lax.axis_index("col")
    c, k = col // 2, col % 2
    x, yh = r // 2, r % 2
    yl, z = c // 4, c % 4
    home = xor(r, swizzle(c), 3)
    slab = swizzle(xor(r, c, 3))
    x_of = {0: x, 1: (x + 3) % 4, 2: (x + 1) % 4, 3: (x + 2) % 4}
    x_ahead = device(x_of[2] * 2 + yh, c, k)
    x_back = device(x_of[1] * 2 + yh, c, k)
    partner = device(x * 2 + 1 - yh, c, k)
    other = device(r, c, 1 - k)

    barrier = pltpu.get_barrier_semaphore()
    senders = [device(c, swizzle(xor(r, c, 3)), k), other, partner, x_ahead, x_back]
    for i in range(1, 8):
        senders.append(device(r, ((yl + i // 4) % 2) * 4 + xor(z, i % 4, 2), k))
    for b in range(8):
        senders.append(device(xor(swizzle(c), b, 3), b, k))
    for s in senders:
        pl.semaphore_signal(barrier, inc=1, device_id=s, device_id_type=MESH)

    own_a = pltpu.make_async_copy(a_ref, a_all.at[k], a_sem.at[0])
    own_a.start()
    own_pat = pltpu.make_async_copy(pat_ref, pat, a_sem.at[1])
    own_pat.start()
    pl.semaphore_wait(barrier, len(senders))

    def remote(src, dst, send, recv, to):
        return pltpu.make_async_remote_copy(
            src_ref=src, dst_ref=dst, send_sem=send, recv_sem=recv, device_id=to, device_id_type=MESH
        )

    stays = jnp.logical_and(r == 0, c == 0)
    halves = [pl.ds(q * HALF, HALF) for q in range(2)]
    first = [
        remote(lt_ref.at[rows], b_all.at[0, rows], first_send.at[q], first_recv.at[q], device(home, r, k))
        for q, rows in enumerate(halves)
    ]

    @pl.when(jnp.logical_not(stays))
    def _():
        for copy in first:
            copy.start()

    @pl.when(stays)
    def _():
        for q, rows in enumerate(halves):
            pltpu.make_async_copy(lt_ref.at[rows], b_all.at[0, rows], first_recv.at[q]).start()

    own_a.wait()
    own_pat.wait()

    def mask(i, carry):
        rows = pl.ds(pl.multiple_of(i * BLK, BLK), BLK)
        for j in range(HALF // BLK):
            keep = jnp.full((BLK, BLK), pat[j, i].astype(F32), F32).astype(BF16)
            cols = slice(j * BLK, (j + 1) * BLK)
            a_all[k, rows, cols] = a_all[k, rows, cols] * keep
        return carry

    lax.fori_loop(0, ROWS // BLK, mask, 0)
    swap = remote(a_all.at[k], a_all.at[k], core_send.at[0], core_recv.at[0], other)
    swap.start()

    def piece(s, q):
        return b_all.at[s, pl.ds(q * HALF, HALF)]

    def along(d, h, q):
        if (d, h) == (3, 1):
            source, to = 6, partner
        else:
            source = {1: h, 2: h, 3: 2 if q == 0 else 4}[d]
            to = x_ahead if d == 1 or (d == 3 and q == 0) else x_back
        i = (d - 1) * 4 + h * 2 + q
        return remote(piece(source, q), piece(2 * d + h, q), x_send.at[i], x_recv.at[i], to)

    def spread(h, q):
        along(1, h, q).start()
        along(2, h, q).start()

    pair = [remote(piece(0, q), piece(1, q), pair_send.at[q], pair_recv.at[q], partner) for q in range(2)]
    for q in range(2):
        first[q].wait_recv()
        spread(0, q)
        pair[q].start()

    remote(a_all.at[1 - k], a_all.at[1 - k], core_send.at[0], core_recv.at[0], other).wait_recv()

    def relation(d, h):
        hi, lo = x_of[d] // 2, x_of[d] % 2
        return hi, ((hi + lo + yl) % 2) * 2 + (yh + h) % 2

    merged = yh == 0
    late_z = [
        jnp.where(x_of[1] // 2 == across, relation(1, 1)[1], relation(2, 1)[1]) for across in range(2)
    ]

    def z_copy(i, t):
        by = i % 4
        if isinstance(i, int):
            hop = by if by != 2 else jnp.where(merged, xor(late_z[i // 4], 2, 2), 2)
        else:
            hop = jnp.where(
                jnp.logical_and(by == 2, merged), xor(jnp.where(i // 4 == 0, late_z[0], late_z[1]), 2, 2), by
            )
        return remote(
            z_out.at[i, with_code(t)], z_in.at[i, with_code(t)], z_send.at[i, t], z_recv.at[i, t],
            device(r, yl * 4 + xor(z, hop, 2), k),
        )

    def y_copy(t):
        return remote(y_out.at[with_code(t)], y_in.at[with_code(t)], y_send.at[t], y_recv.at[t], device(r, (1 - yl) * 4 + z, k))

    def each_tile(body):
        def run(t, carry):
            body(t)
            return carry

        lax.fori_loop(0, TILES, run, 0)


    def packed(values):
        power = code_of(jnp.max(jnp.abs(values), axis=0, keepdims=True))
        code = as_int16(jnp.broadcast_to(power, (CODE, values.shape[1])))
        return as_int16(values * jnp.exp2(power)), code

    def put(ref, t, scaled, code):
        ref[with_code(t), :] = jnp.concatenate([scaled, code], axis=0)

    def unpacked(ref, t):
        ref = ref.at[with_code(t)]
        return as_float(ref[0:size_of(t), :]), unit_of(ref[size_of(t):, :])

    def step(*groups):
        def multiply(t):
            for slots in groups:
                multiply_group(t, slots)

        def multiply_group(t, slots):
            rows = rows_of(t)
            right = [
                jnp.concatenate([b_all[2 * d + h, s, :] for d, h in slots], axis=1)
                for s in (slice(0, HALF), slice(HALF, ROWS))
            ]
            out = jnp.dot(a_all[0, rows, :], right[0], preferred_element_type=F32)
            out = out + jnp.dot(a_all[1, rows, :], right[1], preferred_element_type=F32)
            if slots == LATE:
                held = total.at[0:size_of(t)]
                held[...] = out

                @pl.when(merged)
                def _():
                    for i, slot in enumerate(slots):
                        at = relation(*slot)[0] * 4 + 2
                        cols = slice(i * BLK, (i + 1) * BLK)
                        z_copy(at, t).wait_recv()
                        values, unit = unpacked(z_in.at[at], t)
                        held[:, cols] = held[:, cols] + values * unit

                out = held[...]
            scaled, code = packed(out)
            for i, slot in enumerate(slots):
                across, by = relation(*slot)
                at = across * 4 + by
                cols = slice(i * BLK, (i + 1) * BLK)
                put(z_out.at[at], t, scaled[:, cols], code[:, cols])
                moves = by != 0
                if slot in EARLY:
                    moves = jnp.logical_and(moves, jnp.logical_or(merged, t < KEPT))

                @pl.when(moves)
                def _(at=at):
                    z_copy(at, t).start()

            if (3, 1) in slots:
                for slot in EARLY:
                    across, by = relation(*slot)

                    @pl.when(jnp.logical_and(jnp.logical_and(by != 0, jnp.logical_not(merged)), t < TILES - KEPT))
                    def _(at=across * 4 + by):
                        z_copy(at, t + KEPT).start()

        each_tile(multiply)

    def turned(s, owner):
        part_of = b_turned.at[owner, :, pl.ds(s * BLK, BLK)]
        return remote(part_of, part_of, turn_send.at[s], turn_recv.at[s], other)

    def turn(slots):
        for d, h in slots:
            s = 2 * d + h
            for t in range(TILES):
                b_turned[k, t, s * BLK:(s + 1) * BLK, :] = b_all[s, rows_of(t), :].T
            turned(s, k).start()

    step([(0, 0)])
    along(1, 0, 0).wait_recv()
    along(3, 0, 0).start()
    pair[0].wait_recv()
    spread(1, 0)
    along(2, 0, 1).wait_recv()
    along(3, 0, 1).start()
    pair[1].wait_recv()
    spread(1, 1)
    step([(0, 1)])
    along(1, 0, 1).wait_recv()
    along(2, 0, 0).wait_recv()
    step([(1, 0), (2, 0)])
    for q in range(2):
        along(3, 0, q).wait_recv()
        along(3, 1, q).start()
    step([(3, 0)])
    turn([(0, 0), (0, 1), (1, 0), (2, 0), (3, 0)])
    for d in (1, 2):
        for q in range(2):
            along(d, 1, q).wait_recv()
    turn([(1, 1), (2, 1)])
    for q in range(2):
        along(3, 1, q).wait_recv()
    step(LATE, [(3, 1)])
    turn([(3, 1)])

    def parts_of(across):
        return [z_out.at[across * 4]] + [z_in.at[across * 4 + i] for i in range(1, 4)]

    def sum_of(refs, t):
        out = 0.0
        for i, ref in enumerate(refs):
            values, unit = unpacked(ref, t)
            if i == 2:
                unit = jnp.where(merged, 0.0, unit)
            out = out + values * unit
        return out

    def z_wait(across, t):
        for i in (1, 3):
            z_copy(across * 4 + i, t).wait_recv()

        @pl.when(jnp.logical_not(merged))
        def _():
            z_copy(across * 4 + 2, t).wait_recv()

    def pass_on(t):
        z_wait(1, t)

        put(y_out, t, *packed(sum_of(parts_of(1), t)))
        y_copy(t).start()

    def third(t):
        rows = rows_of(t)
        return remote(mine.at[rows], slabs.at[rows], slab_send.at[t], slab_recv.at[t], device(home, r, k))

    def finish(t):
        z_wait(0, t)

        y_copy(t).wait_recv()
        rows = rows_of(t)
        out = sum_of(parts_of(0) + [y_in], t)
        mine[rows, :] = (-out).astype(BF16)
        panel_ref[rows, :] = (-out).astype(BF16)

        @pl.when(jnp.logical_not(stays))
        def _():
            third(t).start()

        @pl.when(stays)
        def _():
            pltpu.make_async_copy(mine.at[rows], slabs.at[rows], slab_recv.at[t]).start()

    for t in range(TILES + 1):
        if t < TILES:
            pass_on(t)
        if t > 0:
            finish(t - 1)

    for s in range(8):
        turned(s, 1 - k).wait_recv()
    for t in range(TILES):
        third(t).wait_recv()
        right = slabs[rows_of(t), :]
        for kk in range(2):
            for j in range(4):
                span = slice(j * 2 * BLK, (j + 1) * 2 * BLK)
                out = jnp.dot(b_turned[kk, t, span, :], right, preferred_element_type=F32)
                corner[kk, span, :] = out if t == 0 else corner[kk, span, :] + out

    def corner_of(j):
        to = swizzle(xor(x_of[j // 2] * 2 + (yh + j % 2) % 2, c, 3))
        own = jnp.logical_and(to == r, slab == c)
        return own, remote(part.at[j], parts_in.at[c], part_send.at[j], part_recv.at[c], device(to, slab, k))

    for j in range(8):
        span = slice(j * BLK, (j + 1) * BLK)
        scaled, code = packed(jnp.concatenate([corner[0, span, :], corner[1, span, :]], axis=0))
        part[j] = jnp.concatenate([scaled, code], axis=0)
        own, copy = corner_of(j)

        @pl.when(own)
        def _(j=j):
            parts_in[c] = part[j]

        @pl.when(jnp.logical_not(own))
        def _(copy=copy):
            copy.start()

    out = diag_ref[...]
    for b in range(8):
        own = jnp.logical_and(xor(swizzle(c), b, 3) == r, c == b)

        @pl.when(jnp.logical_not(own))
        def _(b=b):
            remote(part.at[0], parts_in.at[b], part_send.at[0], part_recv.at[b], other).wait_recv()

        out = out - as_float(parts_in[b, 0:2 * BLK, :]) * unit_of(parts_in[b, 2 * BLK:, :])
    corner_ref[...] = out

    @pl.when(jnp.logical_not(stays))
    def _():
        for copy in first:
            copy.wait_send()

    swap.wait_send()
    for q in range(2):
        pair[q].wait_send()
        for d in (1, 2, 3):
            for h in range(2):
                along(d, h, q).wait_send()

    def drain(t):
        for i in (1, 2, 3, 5, 6, 7):
            z_copy(i, t).wait_send()


        @pl.when(jnp.logical_not(stays))
        def _():
            third(t).wait_send()

        y_copy(t).wait_send()

    each_tile(drain)
    for j in range(8):
        turned(j, k).wait_send()
        own, copy = corner_of(j)

        @pl.when(jnp.logical_not(own))
        def _(copy=copy):
            copy.wait_send()


def hand_back(panel_ref, corner_ref, panel_out, corner_out, panel_held, corner_held, sem):
    ways = [(corner_ref, corner_held, corner_out)]
    for t in range(TILES):
        rows = pl.ds(t * TILE, TILE)
        ways.append((panel_ref.at[rows], panel_held.at[rows], panel_out.at[rows]))
    reads = [pltpu.make_async_copy(a, b, sem.at[0, i]) for i, (a, b, _) in enumerate(ways)]
    writes = [pltpu.make_async_copy(b, c, sem.at[1, i]) for i, (_, b, c) in enumerate(ways)]
    for copy in reads:
        copy.start()
    for read, write in zip(reads, writes):
        read.wait()
        write.start()
    for copy in writes:
        copy.wait()


def local(selected_inverse, pattern, ltil, diag_inverse):
    dma = pltpu.SemaphoreType.DMA
    vmem, anywhere = pl.BlockSpec(memory_space=pltpu.VMEM), pl.BlockSpec(memory_space=pl.ANY)
    panel, corner = pl.pallas_call(
        kernel,
        out_shape=(
            jax.ShapeDtypeStruct((ROWS, BLK), BF16),
            jax.ShapeDtypeStruct((2 * BLK, BLK), F32),
        ),
        in_specs=[anywhere, anywhere, anywhere, vmem],
        out_specs=(vmem, vmem),
        scratch_shapes=[
            pltpu.SMEM((HALF // BLK, ROWS // BLK), jnp.int32),
            pltpu.VMEM((2, ROWS, HALF), BF16),
            pltpu.VMEM((8, ROWS, BLK), BF16),
            pltpu.VMEM((2, TILES, 8 * BLK, TILE), BF16),
            pltpu.VMEM((TILE, 2 * BLK), F32),
            pltpu.VMEM((8, PACKED, BLK), jnp.int16),
            pltpu.VMEM((8, PACKED, BLK), jnp.int16),
            pltpu.VMEM((PACKED, BLK), jnp.int16),
            pltpu.VMEM((PACKED, BLK), jnp.int16),
            pltpu.VMEM((ROWS, BLK), BF16),
            pltpu.VMEM((ROWS, BLK), BF16),
            pltpu.VMEM((2, 8 * BLK, BLK), F32),
            pltpu.VMEM((8, 2 * BLK + CODE, BLK), jnp.int16),
            pltpu.VMEM((8, 2 * BLK + CODE, BLK), jnp.int16),
            dma((2,)), dma((1,)), dma((1,)), dma((2,)), dma((2,)), dma((2,)), dma((2,)),
            dma((12,)), dma((12,)), dma((8, TILES)), dma((8, TILES)), dma((TILES,)), dma((TILES,)),
            dma((TILES,)), dma((TILES,)), dma((8,)), dma((8,)),
            dma((8,)), dma((8,)),
        ],
        compiler_params=pltpu.CompilerParams(
            collective_id=0, has_side_effects=True, vmem_limit_bytes=56 * 1024 * 1024
        ),
        cost_estimate=pl.CostEstimate(flops=15_000_000_000, bytes_accessed=20_000_000, transcendentals=0),
    )(selected_inverse, pattern.T, ltil, diag_inverse)
    return pl.pallas_call(
        hand_back,
        out_shape=(
            jax.ShapeDtypeStruct((ROWS, BLK), BF16),
            jax.ShapeDtypeStruct((2 * BLK, BLK), F32),
        ),
        in_specs=[anywhere, anywhere],
        out_specs=(anywhere, anywhere),
        scratch_shapes=[
            pltpu.VMEM((ROWS, BLK), BF16),
            pltpu.VMEM((2 * BLK, BLK), F32),
            dma((2, TILES + 1)),
        ],
    )(panel, corner)


def solution(mesh):
    placed = (P("row", "col"), P("row", "col"), P("row", "col"), P("row", "col"))
    return jax.shard_map(
        local,
        mesh=mesh,
        in_specs=placed,
        out_specs=(P("row", "col"), P("row", "col")),
        check_vma=False,
    )
```
